32 devices in a mesh: group: 8 (over z, y), tensor: 4 (over x, core).
Axes of the slice: x: 2, y: 2, z: 4, core: 2. Of those that a mesh axis runs over, the one named last changes fastest.
Arguments:
- query: bfloat16 [2, 256, 2048], P(None, 'group', 'tensor'), may hold values from -80 to 80
- self_kv: bfloat16 [2, 256, 2, 2048], P(None, 'group', None, 'tensor'), may hold values from -6 to 6
- kv_pages: bfloat16 [2, 384, 16, 2, 2048], P(None, 'group', None, None, 'tensor'), may hold values from -6 to 6
- page_dest: int32 [384, 1], replicated, may hold values from 0 to 7; in each aligned block of 48 rows (0 to 47, 48 to 95, ...) at most 12 rows name the same one
- page_request: int32 [384], replicated, may hold values from 0 to 1
- score_len: int32 [16], P('group'), may hold values from 1 to 16
- out_proj: bfloat16 [2, 2048, 2048], P(None, 'tensor'), may hold values from -0.125 to 0.125
- residual: bfloat16 [2, 256, 2048], P(None, ('group', 'tensor')), may hold values from -6 to 6
- norm_gain: float32 [2, 2048], replicated, may hold values from 0.5 to 40
- norm_bias: float32 [2, 2048], replicated, may hold values from -3 to 3
- vocab: bfloat16 [2, 2048, 24576], P(None, None, ('group', 'tensor')), may hold values from -0.3984375 to 0.3984375
- targets: int32 [256], replicated, may hold values from 0 to 24575
Outputs:
- logprob: float32 [2, 256], P(None, ('group', 'tensor'))
The draws below stay inside these ranges and needn't reach their ends.
Inputs may be any that keep to these rules, and one draw needn't show every extreme that they name: `page_dest`: the 48 pages of each aligned block (pages held by one group) go to any one group at most 12 times; some block sends exactly 12 to some group.
All inputs are finite; a program needn't handle non-finite values.
Results may differ from the reference program's by a relative error of at most 0.00097.
Values may be sent and summed in bfloat16 or wider, within the bound.
A program may use at most 192 MiB of HBM per device.

```python
import math
import jax
import jax.numpy as jnp
import numpy as np
from jax import lax

D = 2048
HEADS = 16
HEAD_DIM = 128
REQ_GRP = 2
SCORE_LEN = 16
PAGE = 16
PAGES_DEV = 48
TOK_GRP = 32
TOKENS = 256
REQUESTS = 16
PAGES = 384
CAP = 12
VOCAB = 24576
N_GROUP = 8


def draw_query(key, part):
    first = jax.random.fold_in(key, 0)
    query_shape = (2, TOKENS, HEADS * HEAD_DIM)
    return jnp.clip(jax.random.normal(first, query_shape, jnp.float32), -6.0, 6.0).astype(jnp.bfloat16)


def draw_norm_gain(key, part):
    low_log = math.log(0.5)
    high_log = math.log(2.0)
    return jnp.exp(jax.random.uniform(key, (2, D), jnp.float32, low_log, high_log))


def touch_ends(values, key, smallest, high):
    place = [jax.random.randint(jax.random.fold_in(key, axis), (), 0, length) for axis, length in enumerate(values.shape)]
    longest = values.shape.index(max(values.shape))
    next_to = place[:longest] + [(place[longest] + 1) % values.shape[longest]] + place[longest + 1:]
    return values.at[tuple(place)].set(smallest).at[tuple(next_to)].set(high)


def block_scale(rng, extent, shards, least, high):
    def one(axis_at, blocks):
        steps = jax.random.uniform(jax.random.fold_in(jax.random.fold_in(rng, 6), axis_at), (blocks,), jnp.float32, least / len(shards), high / len(shards))
        return jnp.repeat(jnp.exp(steps), extent[axis_at] // blocks).reshape((-1,) + (1,) * (len(extent) - axis_at - 1))

    gain = one(*shards[0])
    for cut in shards[1:]:
        gain = gain * one(*cut)
    return gain


def rank_table(amount, lean):
    portions = [(1 << 20) // math.isqrt(standing ** lean) + 1 for standing in range(1, amount + 1)]
    spread = 1 + sum(portions) // (1 << 30)
    return np.cumsum(np.array([max(1, weight // spread) for weight in portions]))


def ranked_ids(key, dims, number_of, lean):
    listing = rank_table(number_of, lean)
    ticket = jax.random.randint(jax.random.fold_in(key, 1), dims, 0, int(listing[number_of - 1]))
    standing = jnp.searchsorted(jnp.asarray(listing, jnp.int32), ticket, side="right")
    return jax.random.permutation(jax.random.fold_in(key, 2), number_of)[standing].astype(jnp.int32)


def assign_block(rng, own, number, rows, count, top, reach, slope):
    order = jax.random.permutation(rng, count)
    heavy_load, common = shares(count, rows * top, reach, slope, True), shares(count, rows * top, reach, slope, False)
    places = jnp.arange(count)

    def named(lengths, offset_by):
        used = int((lengths > 0).sum())
        fixed = max(1, used // 4)
        passed = fixed + (places - fixed + offset_by * (used - fixed)) % max(1, count - fixed)
        return jnp.zeros((count,), jnp.int32).at[order[jnp.where(places < fixed, places, passed)]].set(jnp.asarray(lengths, jnp.int32))

    lengths = jnp.where(number % 4 == 0, named(heavy_load, number // 4), named(common, number - number // 4 - 1))
    mixed = jax.random.permutation(jax.random.fold_in(own, 3), count)
    source_of, receiver = mixed[0:count // 2 * 2:2], mixed[1:count // 2 * 2:2]
    slack = jnp.minimum(lengths[source_of] - 1, reach - lengths[receiver]) // 2
    slack = jnp.where((source_of == order[0]) | (receiver == order[0]) | (lengths[receiver] == 0), 0, jnp.maximum(slack, 0))
    passed = jax.random.randint(jax.random.fold_in(own, 4), (count // 2,), 0, 1 << 20) % (slack + 1)
    lengths = lengths.at[source_of].add(-passed).at[receiver].add(passed)
    labels = jnp.searchsorted(jnp.cumsum(lengths), jnp.arange(rows * top), side="right").astype(jnp.int32)
    table = labels.reshape(top, rows).T
    table = table[jax.random.permutation(jax.random.fold_in(own, 1), rows)]
    offset_by = jax.random.randint(jax.random.fold_in(own, 2), (rows, 1), 0, top)
    return jnp.take_along_axis(table, (jnp.arange(top)[None, :] + offset_by) % top, axis=1)


def shares(number_of, total, most, lean, full):
    weights = [(1 << 20) // math.isqrt(rank ** lean) + 1 for rank in range(1, number_of + 1)]
    largest = most if full else min(most, max(-(-total // number_of), total * weights[0] // sum(weights)))
    least = 1 if total - largest >= number_of - 1 else 0
    given, rest = [largest] + [least] * (number_of - 1), total - largest - least * (number_of - 1)
    while rest > 0:
        movable = [i for i in range(1, number_of) if given[i] < largest] or [i for i in range(1, number_of) if given[i] < most]
        mass, budget = sum([weights[i] for i in movable]), rest
        for i in movable:
            more = min(most - given[i], max(1, budget * weights[i] // mass), rest)
            given[i] = given[i] + more
            rest = rest - more
    return np.array(given)


def normal_values(stream_key, shape, scale, limit, pieces=(), kind=jnp.bfloat16):
    loudness = block_scale(stream_key, shape, pieces, -0.22, 0.18) if pieces else 1.0
    entries = jax.random.normal(stream_key, shape, jnp.float32) * scale * loudness
    return jnp.minimum(jnp.maximum(entries, -limit), limit).astype(kind)


def setup_inputs(seed: int = 0) -> dict:
    seeds = jax.random.split(jax.random.key(seed), 13)
    query = draw_query(jax.random.fold_in(seeds[12], 71), 0)
    self_kv = normal_values(seeds[1], (2, TOKENS, 2, HEADS * HEAD_DIM), 1.0, 6.0, ((1, 8), (3, 4)))
    kv_pages = normal_values(seeds[2], (2, PAGES, PAGE, 2, HEADS * HEAD_DIM), 1.0, 6.0, ((1, 8), (4, 4)))
    page_dest_keys = jax.random.split(jax.random.fold_in(seeds[3], 1), PAGES // PAGES_DEV)
    page_dest_turns = jax.random.permutation(jax.random.fold_in(seeds[3], 3), PAGES // PAGES_DEV)
    page_dest = jax.vmap(lambda own, number: assign_block(jax.random.fold_in(seeds[3], 2), own, number, PAGES_DEV, N_GROUP, 1, CAP, 2))(page_dest_keys, page_dest_turns).reshape((PAGES, 1))
    page_request = touch_ends(jax.random.randint(seeds[4], (PAGES,), 0, REQ_GRP), jax.random.fold_in(seeds[4], 1), 0, REQ_GRP - 1).astype(jnp.int32)
    score_len = touch_ends(jax.random.randint(seeds[5], (REQUESTS,), 1, SCORE_LEN + 1), jax.random.fold_in(seeds[5], 1), 1, SCORE_LEN).astype(jnp.int32)
    out_proj = normal_values(seeds[6], (2, HEADS * HEAD_DIM, D), (HEADS * HEAD_DIM) ** -0.5, 0.125, ((1, 4),))
    residual = normal_values(seeds[7], (2, TOKENS, D), 1.0, 6.0, ((1, 32),))
    norm_gain = draw_norm_gain(jax.random.fold_in(seeds[12], 71), 0)
    norm_bias = normal_values(seeds[9], (2, D), 0.5, 3.0, (), jnp.float32)
    vocab = normal_values(seeds[10], (2, D, VOCAB), 0.066, 0.3984375, ((2, 32),))
    targets = touch_ends(ranked_ids(seeds[11], (TOKENS,), VOCAB, 2), jax.random.fold_in(seeds[11], 3), 0, VOCAB - 1).astype(jnp.int32)
    return dict(query=query, self_kv=self_kv, kv_pages=kv_pages, page_dest=page_dest, page_request=page_request, score_len=score_len, out_proj=out_proj, residual=residual, norm_gain=norm_gain, norm_bias=norm_bias, vocab=vocab, targets=targets)


NEGATIVE = -1e+30
EPSILON = 1e-05

def route_tables(destination, request, groups, per_owner, capacity, requests):
    page_count = destination.shape[0]
    owner_group = jnp.arange(page_count, dtype=jnp.int32) // per_owner
    columns = jnp.arange(groups, dtype=jnp.int32)
    onehot = (destination[:, None] == columns[None, :]).astype(jnp.int32)
    within = jnp.cumsum(onehot.reshape(groups, per_owner, groups), axis=1).reshape(page_count, groups)
    position = lax.optimization_barrier(jnp.sum(within * onehot, axis=1)) - 1
    arrival = owner_group * capacity + position
    combined = destination * requests + request
    pair_hot = (combined[:, None] == jnp.arange(groups * requests, dtype=jnp.int32)[None, :]).astype(jnp.int32)
    running = jnp.cumsum(pair_hot, axis=0)
    page_rank = lax.optimization_barrier(jnp.sum(running * pair_hot, axis=1)) - 1
    totals = running[-1].reshape(groups, requests)
    return (position, arrival, page_rank, totals)

def alibi_slopes(head_count):
    return jnp.exp2(-8.0 * jnp.arange(1, head_count + 1).astype(jnp.float32) / head_count)

def group_attention(group_id, query, self_kv, kv_pages, destination, request, arrival, page_rank, totals, slopes):
    tok_grp = TOK_GRP
    buffer = N_GROUP * CAP
    queries = lax.dynamic_slice_in_dim(query, group_id * tok_grp, tok_grp, 1).astype(jnp.float32).reshape(2, tok_grp, HEADS, HEAD_DIM)
    own_kv = lax.dynamic_slice_in_dim(self_kv, group_id * tok_grp, tok_grp, 1).astype(jnp.float32)
    own_keys = own_kv[:, :, 0].reshape(2, tok_grp, HEADS, HEAD_DIM)
    own_values = own_kv[:, :, 1].reshape(2, tok_grp, HEADS, HEAD_DIM)
    target_place = jnp.where(destination == group_id, arrival, buffer)
    slot_index = jnp.full((buffer,), PAGES, jnp.int32).at[target_place].set(jnp.arange(PAGES, dtype=jnp.int32), mode='drop')
    is_valid = slot_index < PAGES
    safe_index = jnp.minimum(slot_index, PAGES - 1)
    page_data = kv_pages[:, safe_index].astype(jnp.float32)
    key_data = page_data[:, :, :, 0].reshape(2, buffer * PAGE, HEADS, HEAD_DIM)
    values = page_data[:, :, :, 1].reshape(2, buffer * PAGE, HEADS, HEAD_DIM)
    key_request = jnp.repeat(jnp.where(is_valid, request[safe_index], -1), PAGE)
    key_position = (page_rank[safe_index][:, None] * PAGE + jnp.arange(PAGE, dtype=jnp.int32)[None, :]).reshape(-1)
    token_ids = jnp.arange(tok_grp, dtype=jnp.int32)
    token_request = token_ids // SCORE_LEN
    token_step = token_ids % SCORE_LEN
    context = totals[group_id][token_request] * PAGE
    distance = (context + token_step)[:, None] - key_position[None, :]
    score_scale = 1.0 / math.sqrt(HEAD_DIM)
    scores = jnp.einsum('mthd,mkhd->mhtk', queries, key_data) * score_scale - slopes[None, :, None, None] * distance.astype(jnp.float32)[None, None]
    allowed = (key_request[None, :] == token_request[:, None])[None, None]
    scores = jnp.where(allowed, scores, NEGATIVE)
    own_distance = (token_step[:, None] - token_step[None, :]).astype(jnp.float32)
    own_scores = jnp.einsum('mthd,mshd->mhts', queries, own_keys) * score_scale - slopes[None, :, None, None] * own_distance[None, None]
    own_allowed = ((token_request[:, None] == token_request[None, :]) & (token_step[None, :] <= token_step[:, None]))[None, None]
    own_scores = jnp.where(own_allowed, own_scores, NEGATIVE)
    row_top = jnp.maximum(lax.optimization_barrier(jnp.max(scores, -1)), lax.optimization_barrier(jnp.max(own_scores, -1)))
    exp_terms = jnp.where(allowed, jnp.exp(scores - row_top[..., None]), 0.0)
    own_terms = jnp.where(own_allowed, jnp.exp(own_scores - row_top[..., None]), 0.0)
    denominator = lax.optimization_barrier(jnp.sum(exp_terms, -1)) + lax.optimization_barrier(jnp.sum(own_terms, -1))
    weights = lax.optimization_barrier(exp_terms.astype(jnp.bfloat16)).astype(jnp.float32)
    own_weights = lax.optimization_barrier(own_terms.astype(jnp.bfloat16)).astype(jnp.float32)
    numerator = jnp.einsum('mhtk,mkhd->mthd', weights, values) + jnp.einsum('mhts,mshd->mthd', own_weights, own_values)
    attended = numerator / jnp.transpose(denominator, (0, 2, 1))[..., None]
    return attended.reshape(2, tok_grp, HEADS * HEAD_DIM).astype(jnp.bfloat16)

def reference(query, self_kv, kv_pages, page_dest, page_request, score_len, out_proj, residual, norm_gain, norm_bias, vocab, targets):
    destination = page_dest[:, 0]
    position, arrival, page_rank, totals = route_tables(destination, page_request, N_GROUP, PAGES_DEV, CAP, REQ_GRP)
    slopes = alibi_slopes(HEADS)

    def one_group(group_id):
        return group_attention(group_id, query, self_kv, kv_pages, destination, page_request, arrival, page_rank, totals, slopes)
    blocks = lax.map(one_group, jnp.arange(N_GROUP, dtype=jnp.int32))
    attended = jnp.transpose(blocks, (1, 0, 2, 3)).reshape(2, TOKENS, HEADS * HEAD_DIM)
    hidden = residual.astype(jnp.float32) + jnp.einsum('mtk,mkd->mtd', attended.astype(jnp.float32), out_proj.astype(jnp.float32))
    row_mean = lax.optimization_barrier(jnp.mean(hidden, axis=-1, keepdims=True))
    centered = hidden - row_mean
    variance = lax.optimization_barrier(jnp.mean(centered * centered, axis=-1, keepdims=True))
    normed = (centered / jnp.sqrt(variance + EPSILON) * norm_gain[:, None, :] + norm_bias[:, None, :]).astype(jnp.bfloat16)

    def score_block(group_id):
        row_block = lax.dynamic_slice_in_dim(normed, group_id * TOK_GRP, TOK_GRP, 1)
        wanted = lax.dynamic_slice_in_dim(targets, group_id * TOK_GRP, TOK_GRP, 0)
        results = []
        for which_model in range(2):
            logits = jnp.dot(row_block[which_model], vocab[which_model], preferred_element_type=jnp.float32)
            row_peak = lax.optimization_barrier(jnp.max(logits, axis=1))
            log_total = row_peak + jnp.log(lax.optimization_barrier(jnp.sum(jnp.exp(logits - row_peak[:, None]), axis=1)))
            chosen = jnp.take_along_axis(logits, wanted[:, None], axis=1)[:, 0]
            results.append(chosen - log_total)
        return jnp.stack(results, 0)
    scored = lax.map(score_block, jnp.arange(N_GROUP, dtype=jnp.int32))
    logprob_all = jnp.transpose(scored, (1, 0, 2)).reshape(2, TOKENS)
    token_ids = jnp.arange(TOKENS, dtype=jnp.int32)
    keep_token = token_ids % SCORE_LEN < score_len[token_ids // SCORE_LEN]
    return jnp.where(keep_token[None, :], logprob_all, 0.0)
```

```python
import functools
import math

import jax
import jax.numpy as jnp
from jax import lax
from jax.experimental import pallas as pl
from jax.experimental.pallas import tpu as pltpu
from jax.sharding import PartitionSpec as P

HEADS = 16
HEAD_DIM = 128
REQ_GRP = 2
SCORE_LEN = 16

NEGATIVE = -1e30
EPSILON = 1e-05
LANES = 128
MESH = pl.DeviceIdType.MESH
F32 = jnp.float32
BF16 = jnp.bfloat16


def gather_events(sizes):
    events = [((0,) * len(sizes), -1)]
    for axis, size in enumerate(sizes):
        held = list(events)
        for offset, _ in held:
            for step in range(1, size):
                moved = list(offset)
                moved[axis] = (size - step) % size
                events.append((tuple(moved), axis))
    return events


def forward_blocks(sizes, here, place, to_device, send_sem, recv_sem):
    def owner_of(offset):
        return [lax.rem(here[a] + offset[a], sizes[a]) if offset[a] else here[a] for a in range(len(sizes))]

    def copy(owner, target, sem):
        ref, slot = place(owner)
        return pltpu.make_async_remote_copy(
            src_ref=ref,
            dst_ref=ref,
            send_sem=sem,
            recv_sem=recv_sem.at[slot],
            device_id=to_device(target),
            device_id_type=MESH,
        )

    state = {"sent": 0, "copies": []}

    def step(event):
        offset, via = event
        owner = owner_of(offset)
        if via >= 0:
            copy(owner, here_next, send_sem.at[0]).wait_recv()
        for axis in range(via + 1, len(sizes)):
            for move in range(1, sizes[axis]):
                target = list(here)
                target[axis] = lax.rem(here[axis] + move, sizes[axis])
                out = copy(owner, target, send_sem.at[state["sent"]])
                out.start()
                state["sent"] += 1
                state["copies"].append(out)

    here_next = list(here)
    here_next[-1] = lax.rem(here[-1] + 1, sizes[-1])
    return step, state["copies"]


def kernel(
    groups,
    shards,
    query_ref,
    own_key_ref,
    own_value_ref,
    key_hbm,
    value_hbm,
    key_owner_ref,
    key_place_ref,
    token_place_ref,
    target_ref,
    proj_hbm,
    residual_ref,
    gain_ref,
    bias_ref,
    vocab_hbm,
    out_ref,
    keys,
    values,
    proj,
    vocab,
    all_query,
    part_num,
    part_stat,
    got_num,
    got_stat,
    attended,
    mixed,
    got_mixed,
    normed,
    stats,
    got_stats,
    local_sem,
    query_send,
    query_recv,
    part_send,
    part_recv,
    mixed_send,
    mixed_recv,
    norm_send_a,
    norm_recv_a,
    norm_send_b,
    norm_recv_b,
    stat_send,
    stat_recv,
):
    group = lax.axis_index("group")
    shard = lax.axis_index("tensor")
    devices = groups * shards
    size_x = shards // 2
    size_y = size_x
    size_z = groups // size_y
    at_z, at_y = group // size_y, lax.rem(group, size_y)
    at_x, core = shard // 2, lax.rem(shard, 2)
    me = group * shards + shard
    tok_grp = query_ref.shape[1]
    flat_width = query_ref.shape[2]
    heads = flat_width // HEAD_DIM
    width = gain_ref.shape[1]
    half_width = width // 2
    rows = tok_grp // shards
    rows_two = 2 * rows
    score_scale = 1.0 / math.sqrt(HEAD_DIM)

    loads = [
        pltpu.make_async_copy(key_hbm, keys, local_sem.at[0]),
        pltpu.make_async_copy(value_hbm, values, local_sem.at[1]),
        pltpu.make_async_copy(proj_hbm, proj, local_sem.at[2]),
        pltpu.make_async_copy(vocab_hbm, vocab, local_sem.at[3]),
    ]
    for load in loads:
        load.start()

    barrier = pltpu.get_barrier_semaphore()

    def greet(step, carry):
        other = lax.rem(me + step, devices)
        pl.semaphore_signal(
            barrier, inc=1, device_id=(other // shards, lax.rem(other, shards)), device_id_type=MESH
        )
        return carry

    all_query[group] = query_ref[...]
    lax.fori_loop(1, devices, greet, 0)
    pl.semaphore_wait(barrier, devices - 1)

    def query_place(owner):
        slot = owner[0] * size_y + owner[1]
        return all_query.at[slot], slot

    sizes = (size_z, size_y)
    query_step, query_copies = forward_blocks(
        sizes,
        [at_z, at_y],
        query_place,
        lambda target: (target[0] * size_y + target[1], shard),
        query_send,
        query_recv,
    )
    for event in gather_events(sizes):
        query_step(event)

    def head_slope(head):
        exponent = (shard * heads + head + 1).astype(F32) * (-8.0 / HEADS)
        return jnp.exp2(jnp.full((1, 1), exponent, F32))

    own_row = lax.broadcasted_iota(jnp.int32, (tok_grp, tok_grp), 0)
    own_column = lax.broadcasted_iota(jnp.int32, (tok_grp, tok_grp), 1)
    own_allowed = (own_row // SCORE_LEN == own_column // SCORE_LEN) & (own_column <= own_row)
    own_distance = (own_row - own_column).astype(F32)
    own_parts = {}
    for model in range(2):
        for head in range(heads):
            span = slice(head * HEAD_DIM, (head + 1) * HEAD_DIM)
            scores = lax.dot_general(
                query_ref[model, :, span],
                own_key_ref[model, :, span],
                (((1,), (1,)), ((), ())),
                preferred_element_type=F32,
            )
            scores = scores * score_scale - head_slope(head) * own_distance
            scores = jnp.where(own_allowed, scores, NEGATIVE)
            top = jnp.max(scores, axis=1, keepdims=True)
            terms = jnp.where(own_allowed, jnp.exp(scores - top), 0.0)
            total = jnp.sum(terms, axis=1, keepdims=True)
            number = jnp.dot(
                terms.astype(BF16), own_value_ref[model, :, span], preferred_element_type=F32
            )
            own_parts[model, head] = (top, total, number)

    loads[0].wait()
    loads[1].wait()
    block = min(groups, 8)
    token_count = block * tok_grp
    key_count = keys.shape[1]

    def attend(index, carry):
        first = index * block
        token = lax.broadcasted_iota(jnp.int32, (token_count, 1), 0) + first * tok_grp
        token_owner = token // SCORE_LEN
        place = token_place_ref[pl.ds(pl.multiple_of(first * tok_grp, token_count), token_count), :]
        allowed = token_owner == key_owner_ref[...]
        distance = (place - key_place_ref[...]).astype(F32)
        lane = lax.broadcasted_iota(jnp.int32, (token_count, LANES), 1)
        packed = jnp.zeros((token_count, LANES), F32)
        for model in range(2):
            for head in range(heads):
                span = slice(head * HEAD_DIM, (head + 1) * HEAD_DIM)
                asked = all_query[pl.ds(first, block), model, :, span].reshape(token_count, HEAD_DIM)
                scores = lax.dot_general(
                    asked,
                    keys[model, :, span],
                    (((1,), (1,)), ((), ())),
                    preferred_element_type=F32,
                )
                scores = scores * score_scale - head_slope(head) * distance
                scores = jnp.where(allowed, scores, NEGATIVE)
                top = jnp.max(scores, axis=1, keepdims=True)
                terms = jnp.where(allowed, jnp.exp(scores - top), 0.0)
                total = jnp.sum(terms, axis=1, keepdims=True)
                number = jnp.dot(
                    terms.astype(BF16), values[model, :, span], preferred_element_type=F32
                )
                part_num[pl.ds(first, block), model, :, span] = number.astype(BF16).reshape(
                    block, tok_grp, HEAD_DIM
                )
                column = model * heads + head
                packed = jnp.where(lane == column, top, packed)
                packed = jnp.where(lane == column + 64, total, packed)
        part_stat[pl.ds(first, block)] = packed.reshape(block, tok_grp, LANES)
        return carry

    lax.fori_loop(0, groups // block, attend, 0)

    part_copies = []
    for step in range(1, groups):
        other = lax.rem(group + step, groups)
        for which, (source, landing) in enumerate(((part_num, got_num), (part_stat, got_stat))):
            copy = pltpu.make_async_remote_copy(
                src_ref=source.at[other],
                dst_ref=landing.at[group],
                send_sem=part_send.at[which, step],
                recv_sem=part_recv.at[which, step],
                device_id=(other, shard),
                device_id_type=MESH,
            )
            copy.start()
            part_copies.append(copy)
    for copy in part_copies:
        copy.wait_recv()

    sources = [(part_num, part_stat, group)]
    for step in range(1, groups):
        sources.append((got_num, got_stat, lax.rem(group + step, groups)))
    source_stats = [stat[index] for _, stat, index in sources]
    for model in range(2):
        for head in range(heads):
            span = slice(head * HEAD_DIM, (head + 1) * HEAD_DIM)
            column = model * heads + head
            own_top, own_total, own_number = own_parts[model, head]
            top = own_top
            for stat in source_stats:
                top = jnp.maximum(top, stat[:, column : column + 1])
            scale = jnp.exp(own_top - top)
            total = own_total * scale
            number = own_number * scale
            for stat, (num, _, index) in zip(source_stats, sources):
                scale = jnp.exp(stat[:, column : column + 1] - top)
                total = total + scale * stat[:, column + 64 : column + 65]
                number = number + scale * num[index, model, :, span].astype(F32)
            attended[model, :, span] = (number / total).astype(BF16)

    loads[2].wait()
    row_shard = lax.broadcasted_iota(jnp.int32, (tok_grp, 1), 0) // rows
    for model in range(2):
        product = jnp.dot(attended[model], proj[model], preferred_element_type=F32)
        held = jnp.concatenate([residual_ref[model].astype(F32)] * shards, axis=0)
        product = product + jnp.where(row_shard == shard, held, 0.0)
        for part in range(shards // 2):
            mixed[model, part] = product[part * rows_two : (part + 1) * rows_two]

    mixed_copies = []
    for step in range(1, shards):
        other = lax.rem(shard + step, shards)
        copy = pltpu.make_async_remote_copy(
            src_ref=mixed.at[lax.rem(other, 2), other // 2],
            dst_ref=got_mixed.at[shard],
            send_sem=mixed_send.at[step],
            recv_sem=mixed_recv.at[step],
            device_id=(group, other),
            device_id_type=MESH,
        )
        copy.start()
        mixed_copies.append(copy)
    hidden = mixed[core, at_x]
    for copy in mixed_copies:
        copy.wait_recv()
    for step in range(1, shards):
        hidden = hidden + got_mixed[lax.rem(shard + step, shards)]
    mean = jnp.mean(hidden, axis=1, keepdims=True)
    centered = hidden - mean
    variance = jnp.mean(centered * centered, axis=1, keepdims=True)
    gain = jnp.where(core == 0, gain_ref[0:1, :], gain_ref[1:2, :])
    bias = jnp.where(core == 0, bias_ref[0:1, :], bias_ref[1:2, :])
    result = (centered / jnp.sqrt(variance + EPSILON) * gain + bias).astype(BF16)
    my_slot = group * size_x + at_x
    normed[0, core, my_slot] = result[:, :half_width]
    normed[1, core, my_slot] = result[:, half_width:]

    slots = groups * size_x

    def norm_place_a(owner):
        slot = (owner[0] * size_y + owner[1]) * size_x + owner[2]
        return normed.at[0, owner[3], slot], owner[3] * slots + slot

    def norm_place_b(owner):
        slot = (owner[0] * size_y + owner[2]) * size_x + owner[1]
        return normed.at[1, owner[3], slot], owner[3] * slots + slot

    sizes_a = (size_z, size_y, size_x, 2)
    sizes_b = (size_z, size_x, size_y, 2)
    step_a, copies_a = forward_blocks(
        sizes_a,
        [at_z, at_y, at_x, core],
        norm_place_a,
        lambda to: (to[0] * size_y + to[1], to[2] * 2 + to[3]),
        norm_send_a,
        norm_recv_a,
    )
    step_b, copies_b = forward_blocks(
        sizes_b,
        [at_z, at_x, at_y, core],
        norm_place_b,
        lambda to: (to[0] * size_y + to[2], to[1] * 2 + to[3]),
        norm_send_b,
        norm_recv_b,
    )
    for event_a, event_b in zip(gather_events(sizes_a), gather_events(sizes_b)):
        step_a(event_a)
        step_b(event_b)

    loads[3].wait()
    words = vocab.shape[2]
    tokens = groups * tok_grp
    chunk = min(tokens, 256)
    chunk_slots = chunk // rows_two
    message = stats.shape[1]

    def score(index, carry):
        lane = lax.broadcasted_iota(jnp.int32, (chunk, LANES), 1)
        word = lax.broadcasted_iota(jnp.int32, (chunk, words), 1) + me * words
        packed = jnp.zeros((chunk, LANES), F32)
        wanted = target_ref[pl.ds(pl.multiple_of(index * chunk, chunk), chunk), :]
        for model in range(2):
            left = normed[0, model, pl.ds(index * chunk_slots, chunk_slots)].reshape(chunk, half_width)
            right = normed[1, model, pl.ds(index * chunk_slots, chunk_slots)].reshape(chunk, half_width)
            logits = jnp.dot(left, vocab[model, :half_width], preferred_element_type=F32)
            logits = logits + jnp.dot(right, vocab[model, half_width:], preferred_element_type=F32)
            peak = jnp.max(logits, axis=1, keepdims=True)
            total = jnp.sum(jnp.exp(logits - peak), axis=1, keepdims=True)
            chosen = jnp.sum(jnp.where(word == wanted, logits, 0.0), axis=1, keepdims=True)
            packed = jnp.where(lane == 3 * model, peak, packed)
            packed = jnp.where(lane == 3 * model + 1, total, packed)
            packed = jnp.where(lane == 3 * model + 2, chosen, packed)
        stats[pl.ds(index * (chunk // message), chunk // message)] = packed.reshape(
            chunk // message, message, LANES
        )
        return carry

    lax.fori_loop(0, tokens // chunk, score, 0)

    def stat_copy(step):
        other = lax.rem(me + step, devices)
        return pltpu.make_async_remote_copy(
            src_ref=stats.at[(other * rows) // message],
            dst_ref=got_stats.at[me],
            send_sem=stat_send.at[step],
            recv_sem=stat_recv.at[step],
            device_id=(other // shards, lax.rem(other, shards)),
            device_id_type=MESH,
        )

    def stat_start(step, carry):
        stat_copy(step).start()
        return carry

    def stat_finish(step, carry):
        stat_copy(step).wait()
        return carry

    lax.fori_loop(1, devices, stat_start, 0)
    got_stats[me] = stats[(me * rows) // message]
    for copy in query_copies + part_copies + mixed_copies + copies_a + copies_b:
        copy.wait_send()
    lax.fori_loop(1, devices, stat_finish, 0)

    gathered = got_stats[...]
    lane = lax.broadcasted_iota(jnp.int32, (message, LANES), 1)
    result = jnp.zeros((message, LANES), F32)
    for model in range(2):
        peaks = gathered[:, :, 3 * model : 3 * model + 1]
        peak = jnp.max(peaks, axis=0)
        total = jnp.sum(
            gathered[:, :, 3 * model + 1 : 3 * model + 2] * jnp.exp(peaks - peak[None]), axis=0
        )
        chosen = jnp.sum(gathered[:, :, 3 * model + 2 : 3 * model + 3], axis=0)
        result = jnp.where(lane == model, chosen - (peak + jnp.log(total)), result)
    out_ref[...] = result


def per_device(
    query,
    self_kv,
    kv_pages,
    page_dest,
    page_request,
    score_len,
    out_proj,
    residual,
    norm_gain,
    norm_bias,
    vocab,
    targets,
):
    groups = lax.axis_size("group")
    shards = lax.axis_size("tensor")
    group_id = lax.axis_index("group")
    tensor_id = lax.axis_index("tensor")
    devices = groups * shards
    tok_grp = query.shape[1]
    flat_width = query.shape[2]
    heads = flat_width // HEAD_DIM
    per_owner = kv_pages.shape[1]
    page_len = kv_pages.shape[2]
    width = out_proj.shape[2]
    words = vocab.shape[2]
    page_total = page_dest.shape[0]
    tokens = groups * tok_grp
    rows = tok_grp // shards
    message = max(8, rows)
    key_count = per_owner * page_len

    combined = page_dest[:, 0] * REQ_GRP + page_request
    page_ids = jnp.arange(page_total, dtype=jnp.int32)
    key_ids = jnp.arange(key_count, dtype=jnp.int32)
    my_combined = lax.dynamic_slice_in_dim(combined, group_id * per_owner, per_owner)
    key_owner = jnp.repeat(my_combined, page_len)
    key_page = group_id * per_owner + key_ids // page_len
    earlier = (combined[:, None] == key_owner[None, :]) & (page_ids[:, None] < key_page[None, :])
    key_place = jnp.sum(earlier.astype(jnp.int32), axis=0) * page_len + key_ids % page_len
    token_ids = jnp.arange(tokens, dtype=jnp.int32)
    seen = (combined[None, :] == (token_ids // SCORE_LEN)[:, None]).astype(jnp.int32)
    token_place = jnp.sum(seen, axis=1) * page_len + token_ids % SCORE_LEN

    keys = kv_pages[:, :, :, 0].reshape(2, key_count, flat_width)
    values = kv_pages[:, :, :, 1].reshape(2, key_count, flat_width)

    vmem = pl.BlockSpec(memory_space=pltpu.VMEM)
    hbm = pl.BlockSpec(memory_space=pl.ANY)
    dma = pltpu.SemaphoreType.DMA
    result = pl.pallas_call(
        functools.partial(kernel, groups, shards),
        out_shape=jax.ShapeDtypeStruct((message, LANES), F32),
        in_specs=[vmem, vmem, vmem, hbm, hbm, vmem, vmem, vmem, vmem, hbm, vmem, vmem, vmem, hbm],
        out_specs=vmem,
        scratch_shapes=[
            pltpu.VMEM((2, key_count, flat_width), BF16),
            pltpu.VMEM((2, key_count, flat_width), BF16),
            pltpu.VMEM(out_proj.shape, BF16),
            pltpu.VMEM(vocab.shape, BF16),
            pltpu.VMEM((groups, 2, tok_grp, flat_width), BF16),
            pltpu.VMEM((groups, 2, tok_grp, flat_width), BF16),
            pltpu.VMEM((groups, tok_grp, LANES), F32),
            pltpu.VMEM((groups, 2, tok_grp, flat_width), BF16),
            pltpu.VMEM((groups, tok_grp, LANES), F32),
            pltpu.VMEM((2, tok_grp, flat_width), BF16),
            pltpu.VMEM((2, shards // 2, 2 * rows, width), F32),
            pltpu.VMEM((shards, 2 * rows, width), F32),
            pltpu.VMEM((2, 2, devices // 2, 2 * rows, width // 2), BF16),
            pltpu.VMEM((tokens // message, message, LANES), F32),
            pltpu.VMEM((devices, message, LANES), F32),
            dma((4,)),
            dma((groups,)),
            dma((groups,)),
            dma((2, groups)),
            dma((2, groups)),
            dma((shards,)),
            dma((shards,)),
            dma((devices,)),
            dma((devices,)),
            dma((devices,)),
            dma((devices,)),
            dma((devices,)),
            dma((devices,)),
        ],
        compiler_params=pltpu.CompilerParams(
            collective_id=0, has_side_effects=True, vmem_limit_bytes=56 * 1024 * 1024
        ),
        name="rollout_logprob",
    )(
        query,
        self_kv[:, :, 0],
        self_kv[:, :, 1],
        keys,
        values,
        key_owner[None, :],
        key_place[None, :],
        token_place[:, None],
        targets[:, None],
        out_proj,
        residual,
        norm_gain,
        norm_bias,
        vocab,
    )
    first = lax.rem(tensor_id * rows, message)
    mine = jnp.transpose(lax.dynamic_slice(result, (first, 0), (rows, 2)))
    local_ids = tensor_id * rows + jnp.arange(rows, dtype=jnp.int32)
    keep_token = local_ids % SCORE_LEN < score_len[local_ids // SCORE_LEN]
    return jnp.where(keep_token[None, :], mine, 0.0)


def solution(mesh):
    in_specs = (
        P(None, "group", "tensor"),
        P(None, "group", None, "tensor"),
        P(None, "group", None, None, "tensor"),
        P(),
        P(),
        P("group"),
        P(None, "tensor", None),
        P(None, ("group", "tensor"), None),
        P(),
        P(),
        P(None, None, ("group", "tensor")),
        P(),
    )
    out_specs = P(None, ("group", "tensor"))
    return jax.shard_map(
        per_device, mesh=mesh, in_specs=in_specs, out_specs=out_specs, check_vma=False
    )
```

```python
import functools
import math

import jax
import jax.numpy as jnp
from jax import lax
from jax.experimental import pallas as pl
from jax.experimental.pallas import tpu as pltpu
from jax.sharding import PartitionSpec as P

HEADS = 16
HEAD_DIM = 128
REQ_GRP = 2
SCORE_LEN = 16

NEGATIVE = -1e30
EPSILON = 1e-05
LANES = 128
MESH = pl.DeviceIdType.MESH
F32 = jnp.float32
BF16 = jnp.bfloat16


def gather_events(sizes):
    events = [((0,) * len(sizes), -1)]
    for axis, size in enumerate(sizes):
        held = list(events)
        for offset, _ in held:
            for step in range(1, size):
                moved = list(offset)
                moved[axis] = (size - step) % size
                events.append((tuple(moved), axis))
    return events


def forward_blocks(sizes, here, place, to_device, send_sem, recv_sem):
    def owner_of(offset):
        return [lax.rem(here[a] + offset[a], sizes[a]) if offset[a] else here[a] for a in range(len(sizes))]

    def copy(owner, target, sem):
        ref, slot = place(owner)
        return pltpu.make_async_remote_copy(
            src_ref=ref,
            dst_ref=ref,
            send_sem=sem,
            recv_sem=recv_sem.at[slot],
            device_id=to_device(target),
            device_id_type=MESH,
        )

    state = {"sent": 0, "copies": []}

    def step(event):
        offset, via = event
        owner = owner_of(offset)
        if via >= 0:
            copy(owner, here_next, send_sem.at[0]).wait_recv()
        for axis in range(via + 1, len(sizes)):
            for move in range(1, sizes[axis]):
                target = list(here)
                target[axis] = lax.rem(here[axis] + move, sizes[axis])
                out = copy(owner, target, send_sem.at[state["sent"]])
                out.start()
                state["sent"] += 1
                state["copies"].append(out)

    here_next = list(here)
    here_next[-1] = lax.rem(here[-1] + 1, sizes[-1])
    return step, state["copies"]


def split_pairs(pairs):
    count = pairs.shape[0]
    row = lax.broadcasted_iota(jnp.int32, (count, count), 0)
    column = lax.broadcasted_iota(jnp.int32, (count, count), 1)
    wanted = jnp.where(row < count // 2, 2 * row, 2 * row - count + 1)
    chooser = jnp.where(column == wanted, 1.0, 0.0).astype(BF16)
    return jnp.dot(chooser, pairs, preferred_element_type=F32).astype(BF16)


def to_column(row):
    count = row.shape[1]
    down = lax.broadcasted_iota(jnp.int32, (count, count), 0)
    across = lax.broadcasted_iota(jnp.int32, (count, count), 1)
    return jnp.sum(jnp.where(down == across, row, 0), axis=1, keepdims=True)


def kernel(
    groups,
    shards,
    page_len,
    query_ref,
    own_ref,
    pages_hbm,
    dest_ref,
    request_ref,
    score_len_ref,
    target_ref,
    proj_hbm,
    residual_ref,
    gain_ref,
    bias_ref,
    vocab_hbm,
    out_ref,
    pages,
    keys,
    values,
    proj,
    vocab,
    all_query,
    part_num,
    part_stat,
    got_num,
    got_stat,
    attended,
    mixed,
    got_core,
    got_mixed,
    normed,
    stats,
    got_stats,
    local_sem,
    query_send,
    query_recv,
    part_send,
    part_recv,
    core_send,
    core_recv,
    mixed_send,
    mixed_recv,
    norm_send_a,
    norm_recv_a,
    norm_send_b,
    norm_recv_b,
    stat_send,
    stat_recv,
):
    group = lax.axis_index("group")
    shard = lax.axis_index("tensor")
    devices = groups * shards
    size_x = shards // 2
    size_y = size_x
    size_z = groups // size_y
    at_z, at_y = group // size_y, lax.rem(group, size_y)
    at_x, core = shard // 2, lax.rem(shard, 2)
    me = group * shards + shard
    tok_grp = query_ref.shape[1]
    flat_width = query_ref.shape[2]
    heads = flat_width // HEAD_DIM
    width = gain_ref.shape[1]
    half_width = width // 2
    rows = tok_grp // shards
    rows_two = 2 * rows
    score_scale = 1.0 / math.sqrt(HEAD_DIM)
    key_count = keys.shape[1]

    loads = [
        pltpu.make_async_copy(pages_hbm, pages, local_sem.at[0]),
        pltpu.make_async_copy(proj_hbm, proj, local_sem.at[1]),
        pltpu.make_async_copy(vocab_hbm, vocab, local_sem.at[2]),
    ]
    for load in loads:
        load.start()

    barrier = pltpu.get_barrier_semaphore()

    def greet(step, carry):
        other = lax.rem(me + step, devices)
        pl.semaphore_signal(
            barrier, inc=1, device_id=(other // shards, lax.rem(other, shards)), device_id_type=MESH
        )
        return carry

    def query_slot(z, y):
        return y * size_z + z

    my_query = query_slot(at_z, at_y)
    all_query[my_query] = query_ref[...]
    lax.fori_loop(1, devices, greet, 0)

    page_owner = dest_ref[...] * REQ_GRP + to_column(request_ref[...])
    page_total = page_owner.shape[0]
    page_id = lax.broadcasted_iota(jnp.int32, (page_total, key_count), 0)
    key_id = lax.broadcasted_iota(jnp.int32, (1, key_count), 1)
    key_page = group * (key_count // page_len) + key_id // page_len
    key_owner = jnp.sum(jnp.where(page_id == key_page, page_owner, 0), axis=0, keepdims=True)
    earlier = (page_owner == key_owner) & (page_id < key_page)
    key_rank = jnp.sum(jnp.where(earlier, 1, 0), axis=0, keepdims=True)
    key_place = key_rank * page_len + lax.rem(key_id, page_len)
    request_lanes = -(-groups * REQ_GRP // LANES) * LANES
    request_id = lax.broadcasted_iota(jnp.int32, (page_total, request_lanes), 1)
    request_pages = jnp.sum(
        jnp.where(page_owner == request_id, 1, 0), axis=0, keepdims=True
    )
    wanted_words = to_column(target_ref[...])

    pl.semaphore_wait(barrier, devices - 1)

    def query_place(owner):
        slot = query_slot(owner[0], owner[1])
        return all_query.at[slot], slot

    sizes = (size_z, size_y)
    query_step, query_copies = forward_blocks(
        sizes,
        [at_z, at_y],
        query_place,
        lambda target: (target[0] * size_y + target[1], shard),
        query_send,
        query_recv,
    )
    query_events = gather_events(sizes)
    query_step(query_events[0])

    loads[0].wait()
    for model in range(2):
        for start in range(0, key_count, 128):
            block = split_pairs(pages[model, 2 * start : 2 * start + 256])
            keys[model, start : start + 128] = block[:128]
            values[model, start : start + 128] = block[128:]
    for event in query_events[1:]:
        if event[1] == 0:
            query_step(event)

    def head_slope(head):
        exponent = (shard * heads + head + 1).astype(F32) * (-8.0 / HEADS)
        return jnp.exp2(jnp.full((1, 1), exponent, F32))

    def attend_own():
        own_row = lax.broadcasted_iota(jnp.int32, (tok_grp, tok_grp), 0)
        own_column = lax.broadcasted_iota(jnp.int32, (tok_grp, tok_grp), 1)
        own_allowed = (own_row // SCORE_LEN == own_column // SCORE_LEN) & (own_column <= own_row)
        own_distance = (own_row - own_column).astype(F32)
        own_parts = {}
        for model in range(2):
            own_split = split_pairs(own_ref[model])
            for head in range(heads):
                span = slice(head * HEAD_DIM, (head + 1) * HEAD_DIM)
                scores = lax.dot_general(
                    query_ref[model, :, span],
                    own_split[:tok_grp, span],
                    (((1,), (1,)), ((), ())),
                    preferred_element_type=F32,
                )
                scores = scores * score_scale - head_slope(head) * own_distance
                scores = jnp.where(own_allowed, scores, NEGATIVE)
                top = jnp.max(scores, axis=1, keepdims=True)
                terms = jnp.where(own_allowed, jnp.exp(scores - top), 0.0)
                total = jnp.sum(terms, axis=1, keepdims=True)
                number = jnp.dot(
                    terms.astype(BF16), own_split[tok_grp:, span], preferred_element_type=F32
                )
                own_parts[model, head] = (top, total, number)
        return own_parts

    token_count = size_z * tok_grp

    def attend(y):
        first = y * size_z
        row = lax.broadcasted_iota(jnp.int32, (token_count, 1), 0)
        token_group = (row // tok_grp) * size_y + y
        token_owner = token_group * REQ_GRP + lax.rem(row, tok_grp) // SCORE_LEN
        lane = lax.broadcasted_iota(jnp.int32, (token_count, request_lanes), 1)
        context = jnp.sum(
            jnp.where(lane == token_owner, request_pages, 0), axis=1, keepdims=True
        )
        place = context * page_len + lax.rem(row, SCORE_LEN)
        allowed = token_owner == key_owner
        distance = (place - key_place).astype(F32)
        lane = lax.broadcasted_iota(jnp.int32, (token_count, LANES), 1)
        packed = jnp.zeros((token_count, LANES), F32)
        for model in range(2):
            for head in range(heads):
                span = slice(head * HEAD_DIM, (head + 1) * HEAD_DIM)
                asked = all_query[pl.ds(first, size_z), model, :, span]
                scores = lax.dot_general(
                    asked.reshape(token_count, HEAD_DIM),
                    keys[model, :, span],
                    (((1,), (1,)), ((), ())),
                    preferred_element_type=F32,
                )
                scores = scores * score_scale - head_slope(head) * distance
                scores = jnp.where(allowed, scores, NEGATIVE)
                top = jnp.max(scores, axis=1, keepdims=True)
                terms = jnp.where(allowed, jnp.exp(scores - top), 0.0)
                total = jnp.sum(terms, axis=1, keepdims=True)
                number = jnp.dot(
                    terms.astype(BF16), values[model, :, span], preferred_element_type=F32
                )
                part_num[pl.ds(first, size_z), model, :, span] = number.astype(BF16).reshape(
                    size_z, tok_grp, HEAD_DIM
                )
                column = model * heads + head
                packed = jnp.where(lane == column, top, packed)
                packed = jnp.where(lane == column + 64, total, packed)
        part_stat[pl.ds(first, size_z)] = packed.reshape(size_z, tok_grp, LANES)

    part_copies = []
    for step_y in range(size_y):
        for event in query_events[1:]:
            if event[1] == 1 and event[0][1] == step_y:
                query_step(event)
        y = lax.rem(at_y + step_y, size_y)
        attend(y)
        for step_z in range(size_z):
            if step_y == 0 and step_z == 0:
                continue
            z = lax.rem(at_z + step_z, size_z)
            for which, (source, landing) in enumerate(
                ((part_num, got_num), (part_stat, got_stat))
            ):
                copy = pltpu.make_async_remote_copy(
                    src_ref=source.at[query_slot(z, y)],
                    dst_ref=landing.at[my_query],
                    send_sem=part_send.at[which, step_y * size_z + step_z],
                    recv_sem=part_recv.at[which, step_y * size_z + step_z],
                    device_id=(z * size_y + y, shard),
                    device_id_type=MESH,
                )
                copy.start()
                part_copies.append(copy)
    own_parts = attend_own()
    for copy in part_copies:
        copy.wait_recv()

    sources = [(part_num, part_stat, my_query)]
    for step in range(1, groups):
        sources.append((got_num, got_stat, lax.rem(my_query + step, groups)))
    source_stats = [stat[index] for _, stat, index in sources]
    for model in range(2):
        for head in range(heads):
            span = slice(head * HEAD_DIM, (head + 1) * HEAD_DIM)
            column = model * heads + head
            own_top, own_total, own_number = own_parts[model, head]
            top = own_top
            for stat in source_stats:
                top = jnp.maximum(top, stat[:, column : column + 1])
            scale = jnp.exp(own_top - top)
            total = own_total * scale
            number = own_number * scale
            for stat, (num, _, index) in zip(source_stats, sources):
                scale = jnp.exp(stat[:, column : column + 1] - top)
                total = total + scale * stat[:, column + 64 : column + 65]
                number = number + scale * num[index, model, :, span].astype(F32)
            attended[model, :, span] = (number / total).astype(BF16)

    loads[1].wait()
    row_shard = lax.broadcasted_iota(jnp.int32, (tok_grp, 1), 0) // rows

    def project(model):
        product = jnp.dot(attended[model], proj[model], preferred_element_type=F32)
        held = jnp.concatenate([residual_ref[model].astype(F32)] * shards, axis=0)
        product = product + jnp.where(row_shard == shard, held, 0.0)
        for part in range(size_x):
            mixed[model, part] = product[part * rows_two : (part + 1) * rows_two]

    core_copies = []
    project(1 - core)
    for step in list(range(1, size_x)) + [0]:
        part = lax.rem(at_x + step, size_x)
        copy = pltpu.make_async_remote_copy(
            src_ref=mixed.at[1 - core, part],
            dst_ref=got_core.at[part],
            send_sem=core_send.at[step],
            recv_sem=core_recv.at[step],
            device_id=(group, at_x * 2 + 1 - core),
            device_id_type=MESH,
        )
        copy.start()
        core_copies.append(copy)
    project(core)
    mixed_copies = []
    for step in range(1, size_x):
        part = lax.rem(at_x + step, size_x)
        core_copies[step - 1].wait_recv()
        mixed[core, part] = mixed[core, part] + got_core[part]
        copy = pltpu.make_async_remote_copy(
            src_ref=mixed.at[core, part],
            dst_ref=got_mixed.at[at_x],
            send_sem=mixed_send.at[step],
            recv_sem=mixed_recv.at[step],
            device_id=(group, part * 2 + core),
            device_id_type=MESH,
        )
        copy.start()
        mixed_copies.append(copy)
    core_copies[-1].wait_recv()
    hidden = mixed[core, at_x] + got_core[at_x]
    for copy in mixed_copies:
        copy.wait_recv()
    for step in range(1, size_x):
        hidden = hidden + got_mixed[lax.rem(at_x + step, size_x)]
    mean = jnp.mean(hidden, axis=1, keepdims=True)
    centered = hidden - mean
    variance = jnp.mean(centered * centered, axis=1, keepdims=True)
    gain = jnp.where(core == 0, gain_ref[0:1, :], gain_ref[1:2, :])
    bias = jnp.where(core == 0, bias_ref[0:1, :], bias_ref[1:2, :])
    result = (centered / jnp.sqrt(variance + EPSILON) * gain + bias).astype(BF16)
    my_slot = group * size_x + at_x
    normed[0, core, my_slot] = result[:, :half_width]
    normed[1, core, my_slot] = result[:, half_width:]

    slots = groups * size_x

    def norm_place_a(owner):
        slot = (owner[0] * size_y + owner[1]) * size_x + owner[2]
        return normed.at[0, owner[3], slot], owner[3] * slots + slot

    def norm_place_b(owner):
        slot = (owner[0] * size_y + owner[2]) * size_x + owner[1]
        return normed.at[1, owner[3], slot], owner[3] * slots + slot

    sizes_a = (size_z, size_y, size_x, 2)
    sizes_b = (size_z, size_x, size_y, 2)
    step_a, copies_a = forward_blocks(
        sizes_a,
        [at_z, at_y, at_x, core],
        norm_place_a,
        lambda to: (to[0] * size_y + to[1], to[2] * 2 + to[3]),
        norm_send_a,
        norm_recv_a,
    )
    step_b, copies_b = forward_blocks(
        sizes_b,
        [at_z, at_x, at_y, core],
        norm_place_b,
        lambda to: (to[0] * size_y + to[2], to[1] * 2 + to[3]),
        norm_send_b,
        norm_recv_b,
    )
    paired = list(zip(gather_events(sizes_a), gather_events(sizes_b)))
    for event_a, event_b in paired:
        if event_a[1] < 3:
            step_a(event_a)
            step_b(event_b)

    loads[2].wait()
    words = vocab.shape[2]
    tokens = groups * tok_grp
    chunk = min(tokens, 256)
    chunk_slots = chunk // rows_two
    message = stats.shape[1]
    chunk_messages = chunk // message
    for turn in range(2):
        model = core if turn == 0 else 1 - core
        if turn == 1:
            for event_a, event_b in paired:
                if event_a[1] == 3:
                    step_a(event_a)
                    step_b(event_b)
        for index in range(tokens // chunk):
            lane = lax.broadcasted_iota(jnp.int32, (chunk, LANES), 1)
            word = lax.broadcasted_iota(jnp.int32, (chunk, words), 1) + me * words
            wanted = wanted_words[index * chunk : (index + 1) * chunk]
            span = slice(index * chunk_slots, (index + 1) * chunk_slots)
            left = normed[0, model, span].reshape(chunk, half_width)
            right = normed[1, model, span].reshape(chunk, half_width)
            logits = jnp.dot(left, vocab[model, :half_width], preferred_element_type=F32)
            logits = logits + jnp.dot(right, vocab[model, half_width:], preferred_element_type=F32)
            peak = jnp.max(logits, axis=1, keepdims=True)
            total = jnp.sum(jnp.exp(logits - peak), axis=1, keepdims=True)
            chosen = jnp.sum(jnp.where(word == wanted, logits, 0.0), axis=1, keepdims=True)
            place = slice(index * chunk_messages, (index + 1) * chunk_messages)
            if turn == 0:
                packed = jnp.zeros((chunk, LANES), F32)
            else:
                packed = stats[place].reshape(chunk, LANES)
            packed = jnp.where(lane == 3 * model, peak, packed)
            packed = jnp.where(lane == 3 * model + 1, total, packed)
            packed = jnp.where(lane == 3 * model + 2, chosen, packed)
            stats[place] = packed.reshape(chunk_messages, message, LANES)

    def stat_copy(step):
        other = lax.rem(me + step, devices)
        return pltpu.make_async_remote_copy(
            src_ref=stats.at[(other * rows) // message],
            dst_ref=got_stats.at[me],
            send_sem=stat_send.at[step],
            recv_sem=stat_recv.at[step],
            device_id=(other // shards, lax.rem(other, shards)),
            device_id_type=MESH,
        )

    def stat_start(step, carry):
        stat_copy(step).start()
        return carry

    def stat_finish(step, carry):
        stat_copy(step).wait()
        return carry

    lax.fori_loop(1, devices, stat_start, 0)
    got_stats[me] = stats[(me * rows) // message]
    for copy in query_copies + part_copies + core_copies + mixed_copies + copies_a + copies_b:
        copy.wait_send()
    lax.fori_loop(1, devices, stat_finish, 0)

    gathered = got_stats[...]
    down = lax.broadcasted_iota(jnp.int32, (message, LANES), 0)
    across = lax.broadcasted_iota(jnp.int32, (message, LANES), 1)
    turned = down == across + lax.rem(shard * rows, message)
    local = shard * rows + lax.broadcasted_iota(jnp.int32, (1, LANES), 1)
    limit = jnp.where(local // SCORE_LEN == 0, score_len_ref[0], score_len_ref[1])
    keep = lax.rem(local, SCORE_LEN) < limit
    for model in range(2):
        peaks = gathered[:, :, 3 * model : 3 * model + 1]
        peak = jnp.max(peaks, axis=0)
        total = jnp.sum(
            gathered[:, :, 3 * model + 1 : 3 * model + 2] * jnp.exp(peaks - peak[None]), axis=0
        )
        chosen = jnp.sum(gathered[:, :, 3 * model + 2 : 3 * model + 3], axis=0)
        column = chosen - (peak + jnp.log(total))
        row = jnp.sum(jnp.where(turned, column, 0.0), axis=0, keepdims=True)
        out_ref[model : model + 1, :] = jnp.where(keep, row, 0.0)[:, :rows]


def per_device(
    query,
    self_kv,
    kv_pages,
    page_dest,
    page_request,
    score_len,
    out_proj,
    residual,
    norm_gain,
    norm_bias,
    vocab,
    targets,
):
    groups = lax.axis_size("group")
    shards = lax.axis_size("tensor")
    devices = groups * shards
    tok_grp = query.shape[1]
    flat_width = query.shape[2]
    page_len = kv_pages.shape[2]
    width = out_proj.shape[2]
    tokens = groups * tok_grp
    rows = tok_grp // shards
    message = max(8, rows)
    key_count = kv_pages.shape[1] * page_len
    size_x = shards // 2

    vmem = pl.BlockSpec(memory_space=pltpu.VMEM)
    smem = pl.BlockSpec(memory_space=pltpu.SMEM)
    hbm = pl.BlockSpec(memory_space=pl.ANY)
    dma = pltpu.SemaphoreType.DMA
    return pl.pallas_call(
        functools.partial(kernel, groups, shards, page_len),
        out_shape=jax.ShapeDtypeStruct((2, rows), F32),
        in_specs=[vmem, vmem, hbm, vmem, vmem, smem, vmem, hbm, vmem, vmem, vmem, hbm],
        out_specs=vmem,
        scratch_shapes=[
            pltpu.VMEM((2, 2 * key_count, flat_width), BF16),
            pltpu.VMEM((2, key_count, flat_width), BF16),
            pltpu.VMEM((2, key_count, flat_width), BF16),
            pltpu.VMEM(out_proj.shape, BF16),
            pltpu.VMEM(vocab.shape, BF16),
            pltpu.VMEM((groups, 2, tok_grp, flat_width), BF16),
            pltpu.VMEM((groups, 2, tok_grp, flat_width), BF16),
            pltpu.VMEM((groups, tok_grp, LANES), F32),
            pltpu.VMEM((groups, 2, tok_grp, flat_width), BF16),
            pltpu.VMEM((groups, tok_grp, LANES), F32),
            pltpu.VMEM((2, tok_grp, flat_width), BF16),
            pltpu.VMEM((2, size_x, 2 * rows, width), F32),
            pltpu.VMEM((size_x, 2 * rows, width), F32),
            pltpu.VMEM((size_x, 2 * rows, width), F32),
            pltpu.VMEM((2, 2, devices // 2, 2 * rows, width // 2), BF16),
            pltpu.VMEM((tokens // message, message, LANES), F32),
            pltpu.VMEM((devices, message, LANES), F32),
            dma((3,)),
            dma((groups,)),
            dma((groups,)),
            dma((2, groups)),
            dma((2, groups)),
            dma((size_x,)),
            dma((size_x,)),
            dma((size_x,)),
            dma((size_x,)),
            dma((devices,)),
            dma((devices,)),
            dma((devices,)),
            dma((devices,)),
            dma((devices,)),
            dma((devices,)),
        ],
        compiler_params=pltpu.CompilerParams(
            collective_id=0, has_side_effects=True, vmem_limit_bytes=56 * 1024 * 1024
        ),
        name="rollout_logprob",
    )(
        query,
        self_kv.reshape(2, 2 * tok_grp, flat_width),
        kv_pages.reshape(2, 2 * key_count, flat_width),
        page_dest,
        page_request[None, :],
        score_len,
        targets[None, :],
        out_proj,
        residual,
        norm_gain,
        norm_bias,
        vocab,
    )


def solution(mesh):
    in_specs = (
        P(None, "group", "tensor"),
        P(None, "group", None, "tensor"),
        P(None, "group", None, None, "tensor"),
        P(),
        P(),
        P("group"),
        P(None, "tensor", None),
        P(None, ("group", "tensor"), None),
        P(),
        P(),
        P(None, None, ("group", "tensor")),
        P(),
    )
    out_specs = P(None, ("group", "tensor"))
    return jax.shard_map(
        per_device, mesh=mesh, in_specs=in_specs, out_specs=out_specs, check_vma=False
    )
```

```python
import functools
import math

import jax
import jax.numpy as jnp
from jax import lax
from jax.experimental import pallas as pl
from jax.experimental.pallas import tpu as pltpu
from jax.sharding import PartitionSpec as P

HEADS = 16
HEAD_DIM = 128
REQ_GRP = 2
SCORE_LEN = 16

NEGATIVE = -1e30
EPSILON = 1e-05
UNSEEN = 1e30
LOWEST_TOP = -1e26
LANES = 128
MESH = pl.DeviceIdType.MESH
F32 = jnp.float32
BF16 = jnp.bfloat16


def gather_events(sizes):
    events = [((0,) * len(sizes), -1)]
    for axis, size in enumerate(sizes):
        held = list(events)
        for offset, _ in held:
            for step in range(1, size):
                moved = list(offset)
                moved[axis] = (size - step) % size
                events.append((tuple(moved), axis))
    return events


def forward_blocks(sizes, here, place, to_device, send_sem, recv_sem):
    def owner_of(offset):
        return [lax.rem(here[a] + offset[a], sizes[a]) if offset[a] else here[a] for a in range(len(sizes))]

    def copy(owner, target, sem):
        ref, slot = place(owner)
        return pltpu.make_async_remote_copy(
            src_ref=ref,
            dst_ref=ref,
            send_sem=sem,
            recv_sem=recv_sem.at[slot],
            device_id=to_device(target),
            device_id_type=MESH,
        )

    state = {"sent": 0, "copies": []}

    def step(event):
        offset, via = event
        owner = owner_of(offset)
        if via >= 0:
            copy(owner, here_next, send_sem.at[0]).wait_recv()
        for axis in range(via + 1, len(sizes)):
            for move in range(1, sizes[axis]):
                target = list(here)
                target[axis] = lax.rem(here[axis] + move, sizes[axis])
                out = copy(owner, target, send_sem.at[state["sent"]])
                out.start()
                state["sent"] += 1
                state["copies"].append(out)

    here_next = list(here)
    here_next[-1] = lax.rem(here[-1] + 1, sizes[-1])
    return step, state["copies"]


def to_column(row):
    count = row.shape[1]
    down = lax.broadcasted_iota(jnp.int32, (count, count), 0)
    across = lax.broadcasted_iota(jnp.int32, (count, count), 1)
    return jnp.sum(jnp.where(down == across, row, 0), axis=1, keepdims=True)


def kernel(
    groups,
    shards,
    page_len,
    query_ref,
    own_ref,
    pages_hbm,
    dest_ref,
    request_ref,
    score_len_ref,
    target_ref,
    proj_hbm,
    residual_ref,
    gain_ref,
    bias_ref,
    vocab_hbm,
    out_ref,
    keys,
    values,
    proj,
    vocab,
    all_query,
    part_num,
    part_stat,
    got_num,
    got_stat,
    attended,
    mixed,
    got_core,
    got_mixed,
    normed,
    stats,
    got_stats,
    local_sem,
    query_send,
    query_recv,
    part_send,
    part_recv,
    core_send,
    core_recv,
    mixed_send,
    mixed_recv,
    norm_send_a,
    norm_recv_a,
    norm_send_b,
    norm_recv_b,
    stat_send,
    stat_recv,
):
    group = lax.axis_index("group")
    shard = lax.axis_index("tensor")
    devices = groups * shards
    size_x = shards // 2
    size_y = size_x
    size_z = groups // size_y
    at_z, at_y = group // size_y, lax.rem(group, size_y)
    at_x, core = shard // 2, lax.rem(shard, 2)
    me = group * shards + shard
    tok_grp = query_ref.shape[1]
    flat_width = query_ref.shape[2]
    heads = flat_width // HEAD_DIM
    width = gain_ref.shape[1]
    half_width = width // 2
    rows = tok_grp // shards
    rows_two = 2 * rows
    score_scale = 1.0 / math.sqrt(HEAD_DIM)
    key_count = keys.shape[1] * page_len

    loads = [
        pltpu.make_async_copy(pages_hbm.at[:, :, 0], keys, local_sem.at[0]),
        pltpu.make_async_copy(pages_hbm.at[:, :, 1], values, local_sem.at[3]),
        pltpu.make_async_copy(proj_hbm, proj, local_sem.at[1]),
        pltpu.make_async_copy(vocab_hbm, vocab, local_sem.at[2]),
    ]
    for load in loads:
        load.start()

    barrier = pltpu.get_barrier_semaphore()

    def greet(step, carry):
        other = lax.rem(me + step, devices)
        pl.semaphore_signal(
            barrier, inc=1, device_id=(lax.div(other, shards), lax.rem(other, shards)), device_id_type=MESH
        )
        return carry

    def query_slot(z, y):
        return y * size_z + z

    my_query = query_slot(at_z, at_y)
    all_query[my_query] = query_ref[...]
    lax.fori_loop(1, devices, greet, 0)

    requests = jnp.concatenate(
        [request_ref[line : line + 1, :] for line in range(request_ref.shape[0])], axis=1
    )
    page_owner = to_column(dest_ref[...] * REQ_GRP + requests)
    page_total = page_owner.shape[0]
    page_id = lax.broadcasted_iota(jnp.int32, (page_total, key_count), 0)
    key_id = lax.broadcasted_iota(jnp.int32, (1, key_count), 1)
    key_page = group * (key_count // page_len) + key_id // page_len
    key_owner = jnp.sum(jnp.where(page_id == key_page, page_owner, 0), axis=0, keepdims=True)
    earlier = (page_owner == key_owner) & (page_id < key_page)
    key_rank = jnp.sum(jnp.where(earlier, 1, 0), axis=0, keepdims=True)
    key_place = key_rank * page_len + lax.rem(key_id, page_len)
    request_lanes = -(-groups * REQ_GRP // LANES) * LANES
    request_id = lax.broadcasted_iota(jnp.int32, (page_total, request_lanes), 1)
    request_pages = jnp.sum(
        jnp.where(page_owner == request_id, 1, 0), axis=0, keepdims=True
    )
    wanted_words = to_column(target_ref[...])

    pl.semaphore_wait(barrier, devices - 1)

    def query_place(owner):
        slot = query_slot(owner[0], owner[1])
        return all_query.at[slot], slot

    sizes = (size_z, size_y)
    query_step, query_copies = forward_blocks(
        sizes,
        [at_z, at_y],
        query_place,
        lambda target: (target[0] * size_y + target[1], shard),
        query_send,
        query_recv,
    )
    query_events = gather_events(sizes)
    query_step(query_events[0])

    for event in query_events[1:]:
        if event[1] == 0:
            query_step(event)

    def head_slope(head):
        exponent = (shard * heads + head + 1).astype(F32) * (-8.0 / HEADS)
        return jnp.exp2(jnp.full((1, 1), exponent, F32))

    def attend_own():
        own_row = lax.broadcasted_iota(jnp.int32, (tok_grp, tok_grp), 0)
        own_column = lax.broadcasted_iota(jnp.int32, (tok_grp, tok_grp), 1)
        own_allowed = (own_row // SCORE_LEN == own_column // SCORE_LEN) & (own_column <= own_row)
        own_distance = (own_row - own_column).astype(F32)
        own_parts = {}
        for model in range(2):
            own_keys = own_ref[model, :, 0, :]
            own_values = own_ref[model, :, 1, :]
            for head in range(heads):
                span = slice(head * HEAD_DIM, (head + 1) * HEAD_DIM)
                scores = lax.dot_general(
                    query_ref[model, :, span],
                    own_keys[:, span],
                    (((1,), (1,)), ((), ())),
                    preferred_element_type=F32,
                )
                scores = scores * score_scale - head_slope(head) * own_distance
                scores = jnp.where(own_allowed, scores, NEGATIVE)
                top = jnp.max(scores, axis=1, keepdims=True)
                terms = jnp.where(own_allowed, jnp.exp(scores - top), 0.0)
                total = jnp.sum(terms, axis=1, keepdims=True)
                number = jnp.dot(
                    terms.astype(BF16), own_values[:, span], preferred_element_type=F32
                )
                own_parts[model, head] = (top, total, number)
        return own_parts

    token_count = size_z * tok_grp

    def attend(y):
        first = y * size_z
        row = lax.broadcasted_iota(jnp.int32, (token_count, 1), 0)
        token_group = (row // tok_grp) * size_y + y
        token_owner = token_group * REQ_GRP + lax.rem(row, tok_grp) // SCORE_LEN
        lane = lax.broadcasted_iota(jnp.int32, (token_count, request_lanes), 1)
        context = jnp.sum(
            jnp.where(lane == token_owner, request_pages, 0), axis=1, keepdims=True
        )
        place = context * page_len + lax.rem(row, SCORE_LEN)
        allowed = token_owner == key_owner
        distance = jnp.where(allowed, (place - key_place).astype(F32), UNSEEN)
        lane = lax.broadcasted_iota(jnp.int32, (token_count, LANES), 1)
        packed = jnp.zeros((token_count, LANES), F32)
        for model in range(2):
            for head in range(heads):
                span = slice(head * HEAD_DIM, (head + 1) * HEAD_DIM)
                asked = all_query[pl.ds(first, size_z), model, :, span]
                scores = lax.dot_general(
                    asked.reshape(token_count, HEAD_DIM),
                    keys[model, :, :, span].reshape(key_count, HEAD_DIM),
                    (((1,), (1,)), ((), ())),
                    preferred_element_type=F32,
                )
                scores = scores * score_scale - head_slope(head) * distance
                top = jnp.maximum(jnp.max(scores, axis=1, keepdims=True), LOWEST_TOP)
                terms = jnp.exp(scores - top)
                total = jnp.sum(terms, axis=1, keepdims=True)
                number = jnp.dot(
                    terms.astype(BF16),
                    values[model, :, :, span].reshape(key_count, HEAD_DIM),
                    preferred_element_type=F32,
                )
                part_num[pl.ds(first, size_z), model, :, span] = number.astype(BF16).reshape(
                    size_z, tok_grp, HEAD_DIM
                )
                column = model * heads + head
                packed = jnp.where(lane == column, top, packed)
                packed = jnp.where(lane == column + 64, total, packed)
        part_stat[pl.ds(first, size_z)] = packed.reshape(size_z, tok_grp, LANES)

    loads[0].wait()
    loads[1].wait()

    part_copies = []
    for step_y in range(size_y):
        for event in query_events[1:]:
            if event[1] == 1 and event[0][1] == step_y:
                query_step(event)
        y = lax.rem(at_y + step_y, size_y)
        attend(y)
        for step_z in range(size_z):
            if step_y == 0 and step_z == 0:
                continue
            z = lax.rem(at_z + step_z, size_z)
            for which, (source, landing) in enumerate(
                ((part_num, got_num), (part_stat, got_stat))
            ):
                copy = pltpu.make_async_remote_copy(
                    src_ref=source.at[query_slot(z, y)],
                    dst_ref=landing.at[my_query],
                    send_sem=part_send.at[which, step_y * size_z + step_z],
                    recv_sem=part_recv.at[which, step_y * size_z + step_z],
                    device_id=(z * size_y + y, shard),
                    device_id_type=MESH,
                )
                copy.start()
                part_copies.append(copy)
    own_parts = attend_own()
    for copy in part_copies:
        copy.wait_recv()

    sources = [(part_num, part_stat, my_query)]
    for step in range(1, groups):
        sources.append((got_num, got_stat, lax.rem(my_query + step, groups)))
    source_stats = [stat[index] for _, stat, index in sources]
    for model in range(2):
        for head in range(heads):
            span = slice(head * HEAD_DIM, (head + 1) * HEAD_DIM)
            column = model * heads + head
            own_top, own_total, own_number = own_parts[model, head]
            top = own_top
            for stat in source_stats:
                top = jnp.maximum(top, stat[:, column : column + 1])
            scale = jnp.exp(own_top - top)
            total = own_total * scale
            number = own_number * scale
            for stat, (num, _, index) in zip(source_stats, sources):
                scale = jnp.exp(stat[:, column : column + 1] - top)
                total = total + scale * stat[:, column + 64 : column + 65]
                number = number + scale * num[index, model, :, span].astype(F32)
            attended[model, :, span] = (number / total).astype(BF16)

    loads[2].wait()
    row_shard = lax.broadcasted_iota(jnp.int32, (tok_grp, 1), 0) // rows

    def project(model):
        product = jnp.dot(attended[model], proj[model], preferred_element_type=F32)
        held = jnp.concatenate([residual_ref[model].astype(F32)] * shards, axis=0)
        product = product + jnp.where(row_shard == shard, held, 0.0)
        for part in range(size_x):
            mixed[model, part] = product[part * rows_two : (part + 1) * rows_two]

    core_copies = []
    project(1 - core)
    for step in list(range(1, size_x)) + [0]:
        part = lax.rem(at_x + step, size_x)
        copy = pltpu.make_async_remote_copy(
            src_ref=mixed.at[1 - core, part],
            dst_ref=got_core.at[part],
            send_sem=core_send.at[step],
            recv_sem=core_recv.at[step],
            device_id=(group, at_x * 2 + 1 - core),
            device_id_type=MESH,
        )
        copy.start()
        core_copies.append(copy)
    project(core)
    mixed_copies = []
    for step in range(1, size_x):
        part = lax.rem(at_x + step, size_x)
        core_copies[step - 1].wait_recv()
        mixed[core, part] = mixed[core, part] + got_core[part]
        copy = pltpu.make_async_remote_copy(
            src_ref=mixed.at[core, part],
            dst_ref=got_mixed.at[at_x],
            send_sem=mixed_send.at[step],
            recv_sem=mixed_recv.at[step],
            device_id=(group, part * 2 + core),
            device_id_type=MESH,
        )
        copy.start()
        mixed_copies.append(copy)
    core_copies[-1].wait_recv()
    hidden = mixed[core, at_x] + got_core[at_x]
    for copy in mixed_copies:
        copy.wait_recv()
    for step in range(1, size_x):
        hidden = hidden + got_mixed[lax.rem(at_x + step, size_x)]
    mean = jnp.mean(hidden, axis=1, keepdims=True)
    centered = hidden - mean
    variance = jnp.mean(centered * centered, axis=1, keepdims=True)
    gain = jnp.where(core == 0, gain_ref[0:1, :], gain_ref[1:2, :])
    bias = jnp.where(core == 0, bias_ref[0:1, :], bias_ref[1:2, :])
    result = (centered / jnp.sqrt(variance + EPSILON) * gain + bias).astype(BF16)
    my_slot = group * size_x + at_x
    normed[0, core, my_slot] = result[:, :half_width]
    normed[1, core, my_slot] = result[:, half_width:]

    slots = groups * size_x

    def norm_place_a(owner):
        slot = (owner[0] * size_y + owner[1]) * size_x + owner[2]
        return normed.at[0, owner[3], slot], owner[3] * slots + slot

    def norm_place_b(owner):
        slot = (owner[0] * size_y + owner[2]) * size_x + owner[1]
        return normed.at[1, owner[3], slot], owner[3] * slots + slot

    sizes_a = (size_z, size_y, size_x, 2)
    sizes_b = (size_z, size_x, size_y, 2)
    step_a, copies_a = forward_blocks(
        sizes_a,
        [at_z, at_y, at_x, core],
        norm_place_a,
        lambda to: (to[0] * size_y + to[1], to[2] * 2 + to[3]),
        norm_send_a,
        norm_recv_a,
    )
    step_b, copies_b = forward_blocks(
        sizes_b,
        [at_z, at_x, at_y, core],
        norm_place_b,
        lambda to: (to[0] * size_y + to[2], to[1] * 2 + to[3]),
        norm_send_b,
        norm_recv_b,
    )
    paired = list(zip(gather_events(sizes_a), gather_events(sizes_b)))
    for event_a, event_b in paired:
        if event_a[1] < 3:
            step_a(event_a)
            step_b(event_b)

    loads[3].wait()
    words = vocab.shape[2]
    tokens = groups * tok_grp
    chunk = min(tokens, 256)
    chunk_slots = chunk // rows_two
    message = stats.shape[1]
    chunk_messages = chunk // message
    for turn in range(2):
        model = core if turn == 0 else 1 - core
        if turn == 1:
            for event_a, event_b in paired:
                if event_a[1] == 3:
                    step_a(event_a)
                    step_b(event_b)
        for index in range(tokens // chunk):
            lane = lax.broadcasted_iota(jnp.int32, (chunk, LANES), 1)
            word = lax.broadcasted_iota(jnp.int32, (chunk, words), 1) + me * words
            wanted = wanted_words[index * chunk : (index + 1) * chunk]
            span = slice(index * chunk_slots, (index + 1) * chunk_slots)
            left = normed[0, model, span].reshape(chunk, half_width)
            right = normed[1, model, span].reshape(chunk, half_width)
            logits = jnp.dot(left, vocab[model, :half_width], preferred_element_type=F32)
            logits = logits + jnp.dot(right, vocab[model, half_width:], preferred_element_type=F32)
            peak = jnp.max(logits, axis=1, keepdims=True)
            total = jnp.sum(jnp.exp(logits - peak), axis=1, keepdims=True)
            chosen = jnp.sum(jnp.where(word == wanted, logits, 0.0), axis=1, keepdims=True)
            place = slice(index * chunk_messages, (index + 1) * chunk_messages)
            if turn == 0:
                packed = jnp.zeros((chunk, LANES), F32)
            else:
                packed = stats[place].reshape(chunk, LANES)
            packed = jnp.where(lane == 3 * model, peak, packed)
            packed = jnp.where(lane == 3 * model + 1, total, packed)
            packed = jnp.where(lane == 3 * model + 2, chosen, packed)
            stats[place] = packed.reshape(chunk_messages, message, LANES)

    def stat_copy(step):
        other = lax.rem(me + step, devices)
        return pltpu.make_async_remote_copy(
            src_ref=stats.at[lax.div(other * rows, message)],
            dst_ref=got_stats.at[me],
            send_sem=stat_send.at[step],
            recv_sem=stat_recv.at[step],
            device_id=(lax.div(other, shards), lax.rem(other, shards)),
            device_id_type=MESH,
        )

    def stat_start(step, carry):
        stat_copy(step).start()
        return carry

    def stat_finish(step, carry):
        stat_copy(step).wait()
        return carry

    lax.fori_loop(1, devices, stat_start, 0)
    got_stats[me] = stats[(me * rows) // message]
    for copy in query_copies + part_copies + core_copies + mixed_copies + copies_a + copies_b:
        copy.wait_send()
    lax.fori_loop(1, devices, stat_finish, 0)

    gathered = got_stats[...]
    down = lax.broadcasted_iota(jnp.int32, (message, LANES), 0)
    across = lax.broadcasted_iota(jnp.int32, (message, LANES), 1)
    turned = down == across + lax.rem(shard * rows, message)
    local = shard * rows + lax.broadcasted_iota(jnp.int32, (1, LANES), 1)
    limit = jnp.where(local // SCORE_LEN == 0, score_len_ref[0], score_len_ref[1])
    keep = lax.rem(local, SCORE_LEN) < limit
    for model in range(2):
        peaks = gathered[:, :, 3 * model : 3 * model + 1]
        peak = jnp.max(peaks, axis=0)
        total = jnp.sum(
            gathered[:, :, 3 * model + 1 : 3 * model + 2] * jnp.exp(peaks - peak[None]), axis=0
        )
        chosen = jnp.sum(gathered[:, :, 3 * model + 2 : 3 * model + 3], axis=0)
        column = chosen - (peak + jnp.log(total))
        row = jnp.sum(jnp.where(turned, column, 0.0), axis=0, keepdims=True)
        out_ref[model : model + 1, :] = jnp.where(keep, row, 0.0)[:, :rows]


def per_device(
    query,
    self_kv,
    kv_pages,
    page_dest,
    page_request,
    score_len,
    out_proj,
    residual,
    norm_gain,
    norm_bias,
    vocab,
    targets,
):
    groups = lax.axis_size("group")
    shards = lax.axis_size("tensor")
    devices = groups * shards
    tok_grp = query.shape[1]
    flat_width = query.shape[2]
    page_len = kv_pages.shape[2]
    width = out_proj.shape[2]
    tokens = groups * tok_grp
    rows = tok_grp // shards
    message = max(8, rows)
    size_x = shards // 2

    vmem = pl.BlockSpec(memory_space=pltpu.VMEM)
    smem = pl.BlockSpec(memory_space=pltpu.SMEM)
    hbm = pl.BlockSpec(memory_space=pl.ANY)
    dma = pltpu.SemaphoreType.DMA
    return pl.pallas_call(
        functools.partial(kernel, groups, shards, page_len),
        out_shape=jax.ShapeDtypeStruct((2, rows), F32),
        in_specs=[vmem, vmem, hbm, vmem, vmem, smem, vmem, hbm, vmem, vmem, vmem, hbm],
        out_specs=vmem,
        scratch_shapes=[
            pltpu.VMEM((2, kv_pages.shape[1], page_len, flat_width), BF16),
            pltpu.VMEM((2, kv_pages.shape[1], page_len, flat_width), BF16),
            pltpu.VMEM(out_proj.shape, BF16),
            pltpu.VMEM(vocab.shape, BF16),
            pltpu.VMEM((groups, 2, tok_grp, flat_width), BF16),
            pltpu.VMEM((groups, 2, tok_grp, flat_width), BF16),
            pltpu.VMEM((groups, tok_grp, LANES), F32),
            pltpu.VMEM((groups, 2, tok_grp, flat_width), BF16),
            pltpu.VMEM((groups, tok_grp, LANES), F32),
            pltpu.VMEM((2, tok_grp, flat_width), BF16),
            pltpu.VMEM((2, size_x, 2 * rows, width), F32),
            pltpu.VMEM((size_x, 2 * rows, width), F32),
            pltpu.VMEM((size_x, 2 * rows, width), F32),
            pltpu.VMEM((2, 2, devices // 2, 2 * rows, width // 2), BF16),
            pltpu.VMEM((tokens // message, message, LANES), F32),
            pltpu.VMEM((devices, message, LANES), F32),
            dma((4,)),
            dma((groups,)),
            dma((groups,)),
            dma((2, groups)),
            dma((2, groups)),
            dma((size_x,)),
            dma((size_x,)),
            dma((size_x,)),
            dma((size_x,)),
            dma((devices,)),
            dma((devices,)),
            dma((devices,)),
            dma((devices,)),
            dma((devices,)),
            dma((devices,)),
        ],
        compiler_params=pltpu.CompilerParams(
            collective_id=0, has_side_effects=True, vmem_limit_bytes=56 * 1024 * 1024
        ),
        name="rollout_logprob",
    )(
        query,
        self_kv,
        jnp.swapaxes(kv_pages, 2, 3),
        jnp.transpose(page_dest),
        page_request.reshape(-1, LANES),
        score_len,
        targets[None, :],
        out_proj,
        residual,
        norm_gain,
        norm_bias,
        vocab,
    )


def solution(mesh):
    in_specs = (
        P(None, "group", "tensor"),
        P(None, "group", None, "tensor"),
        P(None, "group", None, None, "tensor"),
        P(),
        P(),
        P("group"),
        P(None, "tensor", None),
        P(None, ("group", "tensor"), None),
        P(),
        P(),
        P(None, None, ("group", "tensor")),
        P(),
    )
    out_specs = P(None, ("group", "tensor"))
    return jax.shard_map(
        per_device, mesh=mesh, in_specs=in_specs, out_specs=out_specs, check_vma=False
    )
```

```python
import functools
import math

import jax
import jax.numpy as jnp
from jax import lax
from jax.experimental import pallas as pl
from jax.experimental.pallas import tpu as pltpu
from jax.sharding import PartitionSpec as P

HEADS = 16
HEAD_DIM = 128
REQ_GRP = 2
SCORE_LEN = 16

NEGATIVE = -1e30
EPSILON = 1e-05
UNSEEN = 1e30
LOWEST_TOP = -1e26
LANES = 128
MESH = pl.DeviceIdType.MESH
F32 = jnp.float32
BF16 = jnp.bfloat16


def gather_events(sizes):
    events = [((0,) * len(sizes), -1)]
    for axis, size in enumerate(sizes):
        held = list(events)
        for offset, _ in held:
            for step in range(1, size):
                moved = list(offset)
                moved[axis] = (size - step) % size
                events.append((tuple(moved), axis))
    return events


def forward_blocks(sizes, here, place, to_device, send_sem, recv_sem):
    def owner_of(offset):
        return [lax.rem(here[a] + offset[a], sizes[a]) if offset[a] else here[a] for a in range(len(sizes))]

    def copy(owner, target, sem):
        ref, slot = place(owner)
        return pltpu.make_async_remote_copy(
            src_ref=ref,
            dst_ref=ref,
            send_sem=sem,
            recv_sem=recv_sem.at[slot],
            device_id=to_device(target),
            device_id_type=MESH,
        )

    state = {"sent": 0, "copies": []}

    def step(event):
        offset, via = event
        owner = owner_of(offset)
        if via >= 0:
            copy(owner, here_next, send_sem.at[0]).wait_recv()
        for axis in range(via + 1, len(sizes)):
            for move in range(1, sizes[axis]):
                target = list(here)
                target[axis] = lax.rem(here[axis] + move, sizes[axis])
                out = copy(owner, target, send_sem.at[state["sent"]])
                out.start()
                state["sent"] += 1
                state["copies"].append(out)

    here_next = list(here)
    here_next[-1] = lax.rem(here[-1] + 1, sizes[-1])
    return step, state["copies"]


def to_column(row):
    count = row.shape[1]
    down = lax.broadcasted_iota(jnp.int32, (count, count), 0)
    across = lax.broadcasted_iota(jnp.int32, (count, count), 1)
    return jnp.sum(jnp.where(down == across, row, 0), axis=1, keepdims=True)


def kernel(
    groups,
    shards,
    page_len,
    query_ref,
    own_ref,
    pages_hbm,
    dest_ref,
    request_ref,
    score_len_ref,
    target_ref,
    proj_hbm,
    residual_ref,
    gain_ref,
    bias_ref,
    vocab_hbm,
    out_ref,
    keys,
    values,
    proj,
    vocab,
    all_query,
    part_num,
    part_stat,
    got_num,
    got_stat,
    attended,
    mixed,
    got_core,
    got_mixed,
    normed,
    stats,
    got_stats,
    local_sem,
    query_send,
    query_recv,
    part_send,
    part_recv,
    core_send,
    core_recv,
    mixed_send,
    mixed_recv,
    norm_send_a,
    norm_recv_a,
    norm_send_b,
    norm_recv_b,
    stat_send,
    stat_recv,
):
    group = lax.axis_index("group")
    shard = lax.axis_index("tensor")
    devices = groups * shards
    size_x = shards // 2
    size_y = size_x
    size_z = groups // size_y
    at_z, at_y = group // size_y, lax.rem(group, size_y)
    at_x, core = shard // 2, lax.rem(shard, 2)
    me = group * shards + shard
    tok_grp = query_ref.shape[1]
    flat_width = query_ref.shape[2]
    heads = flat_width // HEAD_DIM
    width = gain_ref.shape[1]
    half_width = width // 2
    rows = tok_grp // shards
    rows_two = 2 * rows
    score_scale = 1.0 / math.sqrt(HEAD_DIM)
    key_count = keys.shape[1] * page_len

    loads = [
        pltpu.make_async_copy(pages_hbm.at[:, :, 0], keys, local_sem.at[0]),
        pltpu.make_async_copy(pages_hbm.at[:, :, 1], values, local_sem.at[3]),
        pltpu.make_async_copy(proj_hbm, proj, local_sem.at[1]),
        pltpu.make_async_copy(vocab_hbm, vocab, local_sem.at[2]),
    ]
    for load in loads:
        load.start()

    barrier = pltpu.get_barrier_semaphore()

    def greet(step, carry):
        other = lax.rem(me + step, devices)
        pl.semaphore_signal(
            barrier, inc=1, device_id=(lax.div(other, shards), lax.rem(other, shards)), device_id_type=MESH
        )
        return carry

    def query_slot(z, y):
        return y * size_z + z

    my_query = query_slot(at_z, at_y)
    all_query[my_query] = query_ref[...]
    lax.fori_loop(1, devices, greet, 0)

    requests = jnp.concatenate(
        [request_ref[line : line + 1, :] for line in range(request_ref.shape[0])], axis=1
    )
    page_owner = to_column(dest_ref[...] * REQ_GRP + requests)
    page_total = page_owner.shape[0]
    page_id = lax.broadcasted_iota(jnp.int32, (page_total, key_count), 0)
    key_id = lax.broadcasted_iota(jnp.int32, (1, key_count), 1)
    key_page = group * (key_count // page_len) + key_id // page_len
    key_owner = jnp.sum(jnp.where(page_id == key_page, page_owner, 0), axis=0, keepdims=True)
    earlier = (page_owner == key_owner) & (page_id < key_page)
    key_rank = jnp.sum(jnp.where(earlier, 1, 0), axis=0, keepdims=True)
    key_place = key_rank * page_len + lax.rem(key_id, page_len)
    request_lanes = -(-groups * REQ_GRP // LANES) * LANES
    request_id = lax.broadcasted_iota(jnp.int32, (page_total, request_lanes), 1)
    request_pages = jnp.sum(
        jnp.where(page_owner == request_id, 1, 0), axis=0, keepdims=True
    )
    wanted_words = to_column(target_ref[...])

    pl.semaphore_wait(barrier, devices - 1)

    def query_place(owner):
        slot = query_slot(owner[0], owner[1])
        return all_query.at[slot], slot

    sizes = (size_z, size_y)
    query_step, query_copies = forward_blocks(
        sizes,
        [at_z, at_y],
        query_place,
        lambda target: (target[0] * size_y + target[1], shard),
        query_send,
        query_recv,
    )
    query_events = gather_events(sizes)
    query_step(query_events[0])

    for event in query_events[1:]:
        if event[1] == 0:
            query_step(event)

    def head_slope(head):
        exponent = (shard * heads + head + 1).astype(F32) * (-8.0 / HEADS)
        return jnp.exp2(jnp.full((1, 1), exponent, F32))

    def attend_own():
        own_row = lax.broadcasted_iota(jnp.int32, (tok_grp, tok_grp), 0)
        own_column = lax.broadcasted_iota(jnp.int32, (tok_grp, tok_grp), 1)
        own_allowed = (own_row // SCORE_LEN == own_column // SCORE_LEN) & (own_column <= own_row)
        own_distance = (own_row - own_column).astype(F32)
        own_parts = {}
        for model in range(2):
            own_keys = own_ref[model, :, 0, :]
            own_values = own_ref[model, :, 1, :]
            for head in range(heads):
                span = slice(head * HEAD_DIM, (head + 1) * HEAD_DIM)
                scores = lax.dot_general(
                    query_ref[model, :, span],
                    own_keys[:, span],
                    (((1,), (1,)), ((), ())),
                    preferred_element_type=F32,
                )
                scores = scores * score_scale - head_slope(head) * own_distance
                scores = jnp.where(own_allowed, scores, NEGATIVE)
                top = jnp.max(scores, axis=1, keepdims=True)
                terms = jnp.where(own_allowed, jnp.exp(scores - top), 0.0)
                total = jnp.sum(terms, axis=1, keepdims=True)
                number = jnp.dot(
                    terms.astype(BF16), own_values[:, span], preferred_element_type=F32
                )
                own_parts[model, head] = (top, total, number)
        return own_parts

    token_count = size_z * tok_grp

    def attend(y):
        first = y * size_z
        row = lax.broadcasted_iota(jnp.int32, (token_count, 1), 0)
        token_group = (row // tok_grp) * size_y + y
        token_owner = token_group * REQ_GRP + lax.rem(row, tok_grp) // SCORE_LEN
        lane = lax.broadcasted_iota(jnp.int32, (token_count, request_lanes), 1)
        context = jnp.sum(
            jnp.where(lane == token_owner, request_pages, 0), axis=1, keepdims=True
        )
        place = context * page_len + lax.rem(row, SCORE_LEN)
        allowed = token_owner == key_owner
        distance = jnp.where(allowed, (place - key_place).astype(F32), UNSEEN)
        lane = lax.broadcasted_iota(jnp.int32, (size_z, 8, LANES), 2)
        packed = jnp.zeros((size_z, 8, LANES), F32)
        for model in range(2):
            for head in range(heads):
                span = slice(head * HEAD_DIM, (head + 1) * HEAD_DIM)
                asked = all_query[pl.ds(first, size_z), model, :, span]
                scores = lax.dot_general(
                    asked.reshape(token_count, HEAD_DIM),
                    keys[model, :, :, span].reshape(key_count, HEAD_DIM),
                    (((1,), (1,)), ((), ())),
                    preferred_element_type=F32,
                )
                scores = scores * score_scale - head_slope(head) * distance
                top = jnp.maximum(jnp.max(scores, axis=1, keepdims=True), LOWEST_TOP)
                terms = jnp.exp(scores - top)
                total = jnp.sum(terms, axis=1, keepdims=True)
                number = jnp.dot(
                    terms.astype(BF16),
                    values[model, :, :, span].reshape(key_count, HEAD_DIM),
                    preferred_element_type=F32,
                )
                part_num[pl.ds(first, size_z), model, :, span] = number.astype(BF16).reshape(
                    size_z, tok_grp, HEAD_DIM
                )
                column = model * heads + head
                top = top.reshape(size_z, tok_grp // 8, 8, 1)
                total = total.reshape(size_z, tok_grp // 8, 8, 1)
                for eight in range(tok_grp // 8):
                    at = eight * 4 * heads + column
                    packed = jnp.where(lane == at, top[:, eight], packed)
                    packed = jnp.where(lane == at + 2 * heads, total[:, eight], packed)
        part_stat[pl.ds(first, size_z)] = packed

    loads[0].wait()
    loads[1].wait()

    part_copies = []
    for step_y in range(size_y):
        for event in query_events[1:]:
            if event[1] == 1 and event[0][1] == step_y:
                query_step(event)
        y = lax.rem(at_y + step_y, size_y)
        attend(y)
        for step_z in range(size_z):
            if step_y == 0 and step_z == 0:
                continue
            z = lax.rem(at_z + step_z, size_z)
            for which, (source, landing) in enumerate(
                ((part_num, got_num), (part_stat, got_stat))
            ):
                copy = pltpu.make_async_remote_copy(
                    src_ref=source.at[query_slot(z, y)],
                    dst_ref=landing.at[my_query],
                    send_sem=part_send.at[which, step_y * size_z + step_z],
                    recv_sem=part_recv.at[which, step_y * size_z + step_z],
                    device_id=(z * size_y + y, shard),
                    device_id_type=MESH,
                )
                copy.start()
                part_copies.append(copy)
    own_parts = attend_own()
    for copy in part_copies:
        copy.wait_recv()

    sources = [(part_num, part_stat, my_query)]
    for step in range(1, groups):
        sources.append((got_num, got_stat, lax.rem(my_query + step, groups)))
    source_stats = [stat[index] for _, stat, index in sources]

    def stat_column(stat, column):
        places = [eight * 4 * heads + column for eight in range(tok_grp // 8)]
        return jnp.concatenate([stat[:, at : at + 1] for at in places], axis=0)

    for model in range(2):
        for head in range(heads):
            span = slice(head * HEAD_DIM, (head + 1) * HEAD_DIM)
            column = model * heads + head
            own_top, own_total, own_number = own_parts[model, head]
            top = own_top
            source_tops = [stat_column(stat, column) for stat in source_stats]
            for source_top in source_tops:
                top = jnp.maximum(top, source_top)
            scale = jnp.exp(own_top - top)
            total = own_total * scale
            number = own_number * scale
            for source_top, stat, (num, _, index) in zip(source_tops, source_stats, sources):
                scale = jnp.exp(source_top - top)
                total = total + scale * stat_column(stat, column + 2 * heads)
                number = number + scale * num[index, model, :, span].astype(F32)
            attended[model, :, span] = (number / total).astype(BF16)

    loads[2].wait()
    row_shard = lax.broadcasted_iota(jnp.int32, (tok_grp, 1), 0) // rows

    def project(model):
        product = jnp.dot(attended[model], proj[model], preferred_element_type=F32)
        held = jnp.concatenate([residual_ref[model].astype(F32)] * shards, axis=0)
        product = product + jnp.where(row_shard == shard, held, 0.0)
        for part in range(size_x):
            mixed[model, part] = product[part * rows_two : (part + 1) * rows_two]

    core_copies = []
    project(1 - core)
    for step in list(range(1, size_x)) + [0]:
        part = lax.rem(at_x + step, size_x)
        copy = pltpu.make_async_remote_copy(
            src_ref=mixed.at[1 - core, part],
            dst_ref=got_core.at[part],
            send_sem=core_send.at[step],
            recv_sem=core_recv.at[step],
            device_id=(group, at_x * 2 + 1 - core),
            device_id_type=MESH,
        )
        copy.start()
        core_copies.append(copy)
    project(core)
    mixed_copies = []
    for step in range(1, size_x):
        part = lax.rem(at_x + step, size_x)
        core_copies[step - 1].wait_recv()
        mixed[core, part] = mixed[core, part] + got_core[part]
        copy = pltpu.make_async_remote_copy(
            src_ref=mixed.at[core, part],
            dst_ref=got_mixed.at[at_x],
            send_sem=mixed_send.at[step],
            recv_sem=mixed_recv.at[step],
            device_id=(group, part * 2 + core),
            device_id_type=MESH,
        )
        copy.start()
        mixed_copies.append(copy)
    core_copies[-1].wait_recv()
    hidden = mixed[core, at_x] + got_core[at_x]
    for copy in mixed_copies:
        copy.wait_recv()
    for step in range(1, size_x):
        hidden = hidden + got_mixed[lax.rem(at_x + step, size_x)]
    mean = jnp.mean(hidden, axis=1, keepdims=True)
    centered = hidden - mean
    variance = jnp.mean(centered * centered, axis=1, keepdims=True)
    gain = jnp.where(core == 0, gain_ref[0:1, :], gain_ref[1:2, :])
    bias = jnp.where(core == 0, bias_ref[0:1, :], bias_ref[1:2, :])
    result = (centered / jnp.sqrt(variance + EPSILON) * gain + bias).astype(BF16)
    my_slot = group * size_x + at_x
    normed[0, core, my_slot] = result[:, :half_width]
    normed[1, core, my_slot] = result[:, half_width:]

    slots = groups * size_x

    def norm_place_a(owner):
        slot = (owner[0] * size_y + owner[1]) * size_x + owner[2]
        return normed.at[0, owner[3], slot], owner[3] * slots + slot

    def norm_place_b(owner):
        slot = (owner[0] * size_y + owner[2]) * size_x + owner[1]
        return normed.at[1, owner[3], slot], owner[3] * slots + slot

    sizes_a = (size_z, size_y, size_x, 2)
    sizes_b = (size_z, size_x, size_y, 2)
    step_a, copies_a = forward_blocks(
        sizes_a,
        [at_z, at_y, at_x, core],
        norm_place_a,
        lambda to: (to[0] * size_y + to[1], to[2] * 2 + to[3]),
        norm_send_a,
        norm_recv_a,
    )
    step_b, copies_b = forward_blocks(
        sizes_b,
        [at_z, at_x, at_y, core],
        norm_place_b,
        lambda to: (to[0] * size_y + to[2], to[1] * 2 + to[3]),
        norm_send_b,
        norm_recv_b,
    )
    paired = list(zip(gather_events(sizes_a), gather_events(sizes_b)))
    for event_a, event_b in paired:
        if event_a[1] < 3:
            step_a(event_a)
            step_b(event_b)

    loads[3].wait()
    words = vocab.shape[2]
    tokens = groups * tok_grp
    chunk = min(tokens, 256)
    chunk_slots = chunk // rows_two
    message = stats.shape[1]
    chunk_messages = chunk // message
    for turn in range(2):
        model = core if turn == 0 else 1 - core
        if turn == 1:
            for event_a, event_b in paired:
                if event_a[1] == 3:
                    step_a(event_a)
                    step_b(event_b)
        for index in range(tokens // chunk):
            lane = lax.broadcasted_iota(jnp.int32, (chunk, LANES), 1)
            word = lax.broadcasted_iota(jnp.int32, (chunk, words), 1) + me * words
            wanted = wanted_words[index * chunk : (index + 1) * chunk]
            span = slice(index * chunk_slots, (index + 1) * chunk_slots)
            left = normed[0, model, span].reshape(chunk, half_width)
            right = normed[1, model, span].reshape(chunk, half_width)
            logits = jnp.dot(left, vocab[model, :half_width], preferred_element_type=F32)
            logits = logits + jnp.dot(right, vocab[model, half_width:], preferred_element_type=F32)
            peak = jnp.max(logits, axis=1, keepdims=True)
            total = jnp.sum(jnp.exp(logits - peak), axis=1, keepdims=True)
            chosen = jnp.sum(jnp.where(word == wanted, logits, 0.0), axis=1, keepdims=True)
            place = slice(index * chunk_messages, (index + 1) * chunk_messages)
            if turn == 0:
                packed = jnp.zeros((chunk, LANES), F32)
            else:
                packed = stats[place].reshape(chunk, LANES)
            packed = jnp.where(lane == 3 * model, peak, packed)
            packed = jnp.where(lane == 3 * model + 1, total, packed)
            packed = jnp.where(lane == 3 * model + 2, chosen, packed)
            stats[place] = packed.reshape(chunk_messages, message, LANES)

    def stat_copy(step):
        other = lax.rem(me + step, devices)
        return pltpu.make_async_remote_copy(
            src_ref=stats.at[lax.div(other * rows, message)],
            dst_ref=got_stats.at[me],
            send_sem=stat_send.at[step],
            recv_sem=stat_recv.at[step],
            device_id=(lax.div(other, shards), lax.rem(other, shards)),
            device_id_type=MESH,
        )

    def stat_start(step, carry):
        stat_copy(step).start()
        return carry

    def stat_finish(step, carry):
        stat_copy(step).wait()
        return carry

    lax.fori_loop(1, devices, stat_start, 0)
    got_stats[me] = stats[(me * rows) // message]
    for copy in query_copies + part_copies + core_copies + mixed_copies + copies_a + copies_b:
        copy.wait_send()
    lax.fori_loop(1, devices, stat_finish, 0)

    gathered = got_stats[...]
    down = lax.broadcasted_iota(jnp.int32, (message, LANES), 0)
    across = lax.broadcasted_iota(jnp.int32, (message, LANES), 1)
    turned = down == across + lax.rem(shard * rows, message)
    local = shard * rows + lax.broadcasted_iota(jnp.int32, (1, LANES), 1)
    limit = jnp.where(local // SCORE_LEN == 0, score_len_ref[0], score_len_ref[1])
    keep = lax.rem(local, SCORE_LEN) < limit
    for model in range(2):
        peaks = gathered[:, :, 3 * model : 3 * model + 1]
        peak = jnp.max(peaks, axis=0)
        total = jnp.sum(
            gathered[:, :, 3 * model + 1 : 3 * model + 2] * jnp.exp(peaks - peak[None]), axis=0
        )
        chosen = jnp.sum(gathered[:, :, 3 * model + 2 : 3 * model + 3], axis=0)
        column = chosen - (peak + jnp.log(total))
        row = jnp.sum(jnp.where(turned, column, 0.0), axis=0, keepdims=True)
        out_ref[model : model + 1, :] = jnp.where(keep, row, 0.0)[:, :rows]


def per_device(
    query,
    self_kv,
    kv_pages,
    page_dest,
    page_request,
    score_len,
    out_proj,
    residual,
    norm_gain,
    norm_bias,
    vocab,
    targets,
):
    groups = lax.axis_size("group")
    shards = lax.axis_size("tensor")
    devices = groups * shards
    tok_grp = query.shape[1]
    flat_width = query.shape[2]
    page_len = kv_pages.shape[2]
    width = out_proj.shape[2]
    tokens = groups * tok_grp
    rows = tok_grp // shards
    message = max(8, rows)
    size_x = shards // 2

    vmem = pl.BlockSpec(memory_space=pltpu.VMEM)
    smem = pl.BlockSpec(memory_space=pltpu.SMEM)
    hbm = pl.BlockSpec(memory_space=pl.ANY)
    dma = pltpu.SemaphoreType.DMA
    return pl.pallas_call(
        functools.partial(kernel, groups, shards, page_len),
        out_shape=jax.ShapeDtypeStruct((2, rows), F32),
        in_specs=[vmem, vmem, hbm, vmem, vmem, smem, vmem, hbm, vmem, vmem, vmem, hbm],
        out_specs=vmem,
        scratch_shapes=[
            pltpu.VMEM((2, kv_pages.shape[1], page_len, flat_width), BF16),
            pltpu.VMEM((2, kv_pages.shape[1], page_len, flat_width), BF16),
            pltpu.VMEM(out_proj.shape, BF16),
            pltpu.VMEM(vocab.shape, BF16),
            pltpu.VMEM((groups, 2, tok_grp, flat_width), BF16),
            pltpu.VMEM((groups, 2, tok_grp, flat_width), BF16),
            pltpu.VMEM((groups, 8, LANES), F32),
            pltpu.VMEM((groups, 2, tok_grp, flat_width), BF16),
            pltpu.VMEM((groups, 8, LANES), F32),
            pltpu.VMEM((2, tok_grp, flat_width), BF16),
            pltpu.VMEM((2, size_x, 2 * rows, width), F32),
            pltpu.VMEM((size_x, 2 * rows, width), F32),
            pltpu.VMEM((size_x, 2 * rows, width), F32),
            pltpu.VMEM((2, 2, devices // 2, 2 * rows, width // 2), BF16),
            pltpu.VMEM((tokens // message, message, LANES), F32),
            pltpu.VMEM((devices, message, LANES), F32),
            dma((4,)),
            dma((groups,)),
            dma((groups,)),
            dma((2, groups)),
            dma((2, groups)),
            dma((size_x,)),
            dma((size_x,)),
            dma((size_x,)),
            dma((size_x,)),
            dma((devices,)),
            dma((devices,)),
            dma((devices,)),
            dma((devices,)),
            dma((devices,)),
            dma((devices,)),
        ],
        compiler_params=pltpu.CompilerParams(
            collective_id=0, has_side_effects=True, vmem_limit_bytes=56 * 1024 * 1024
        ),
        name="rollout_logprob",
    )(
        query,
        self_kv,
        jnp.swapaxes(kv_pages, 2, 3),
        jnp.transpose(page_dest),
        page_request.reshape(-1, LANES),
        score_len,
        targets[None, :],
        out_proj,
        residual,
        norm_gain,
        norm_bias,
        vocab,
    )


def solution(mesh):
    in_specs = (
        P(None, "group", "tensor"),
        P(None, "group", None, "tensor"),
        P(None, "group", None, None, "tensor"),
        P(),
        P(),
        P("group"),
        P(None, "tensor", None),
        P(None, ("group", "tensor"), None),
        P(),
        P(),
        P(None, None, ("group", "tensor")),
        P(),
    )
    out_specs = P(None, ("group", "tensor"))
    return jax.shard_map(
        per_device, mesh=mesh, in_specs=in_specs, out_specs=out_specs, check_vma=False
    )
```
